1024 devices in a mesh: dp: 64 (over y, x, core), tensor: 16 (over z).
Axes of the slice: x: 4, y: 8, z: 16, core: 2. Of those that a mesh axis runs over, the one named last changes fastest.
Arguments:
- patches: bfloat16 [32768, 1280], P('dp'), may hold values from -6 to 6
- live_blocks: int32 [64], P('dp'), may hold values from 1 to 4, as said below
- owner_map: int32 [8192, 1], P('dp'), may hold values from 0 to 63; in each aligned block of 128 rows (0 to 127, 128 to 255, ...) at most 2 rows name the same one
- vit_gain: float32 [1280], replicated, may hold values from 0.1 to 1.9
- fc1_weight: bfloat16 [1280, 5120], P(None, 'tensor'), may hold values from -0.15625 to 0.15625
- fc2_weight: bfloat16 [5120, 1280], P('tensor'), may hold values from -0.078125 to 0.078125
- merge_gain: float32 [1280], replicated, may hold values from 0.1 to 1.9
- mid_weight: bfloat16 [5120, 5120], P(None, 'tensor'), may hold values from -0.078125 to 0.078125
- proj_weight: bfloat16 [5120, 4096], P('tensor'), may hold values from -0.125 to 0.125
Outputs:
- llm_embeds: bfloat16 [8192, 4096], P('dp', 'tensor')
The draws below stay inside these ranges and needn't reach their ends.
Inputs may be any that keep to these rules, and one draw needn't show every extreme that they name: `live_blocks`: each rank holds at least one live block; ranks 0, 31, 32 and 63 hold 4, and some rank between 1 and 30 holds one. `owner_map`: among the 128 rows of one rank no owner is named more than 2 times, and some owner exactly that often.
All inputs are finite; a program needn't handle non-finite values.
Results may differ from the reference program's by a relative error of at most 0.0095.
Values may be sent and summed in bfloat16 or wider, within the bound.
A program may use at most 64 MiB of HBM per device.

```python
import math
import jax
import jax.numpy as jnp
import numpy as np
from jax import lax

D = 1280
FF = 5120
EMB = 4096
SLOTS = 4
BLK = 128
MERGED = 128
CAP_OWN = 2
N_DP = 64


def draw_live_blocks(key, part):
    key = jax.random.fold_in(key, 7)
    first, second = jax.random.split(key, 2)
    pick = jax.random.randint(first, (N_DP,), 0, 12)
    counts = jnp.where(pick == 0, SLOTS, jnp.where(pick == 1, 2, 1))
    light = 1 + jax.random.randint(second, (), 0, N_DP // 2 - 2)
    counts = counts.at[light].set(1)
    counts = counts.at[0].set(SLOTS)
    counts = counts.at[N_DP // 2 - 1].set(SLOTS)
    counts = counts.at[N_DP // 2].set(SLOTS)
    counts = counts.at[N_DP - 1].set(SLOTS)
    return counts.astype(jnp.int32)


def spiked(values, key, source, target, blocks, factor):
    owner, partner = [(jnp.arange(values.shape[position]) // (values.shape[position] // blocks)).reshape([-1 if axis == position else 1 for axis in range(values.ndim)]) for position in (source, target)]
    chosen = jax.random.permutation(key, blocks)[partner]
    strong = (owner == chosen) | (owner == (partner + blocks // 2) % blocks)
    return jnp.where(strong, factor * values, values)


def shard_levels(key, extent, cuts, least, high):
    level = 1.0
    for dim, parts in cuts:
        heights = jax.random.uniform(jax.random.fold_in(jax.random.fold_in(key, 6), dim), (parts,), jnp.float32, least / len(cuts), high / len(cuts))
        level = level * jnp.repeat(jnp.exp(heights), extent[dim] // parts).reshape((-1,) + (1,) * (len(extent) - 1 - dim))
    return level


def routed_block(key, own, number, rows, count, top, reach, slope):
    sequence = jax.random.permutation(key, count)
    heavy_load, ordinary = portions_of(count, rows * top, reach, slope, True), portions_of(count, rows * top, reach, slope, False)
    places = jnp.arange(count)

    def named(lengths, offset_by):
        used = int((lengths > 0).sum())
        fixed = max(1, used // 4)
        moved = fixed + (places - fixed + offset_by * (used - fixed)) % max(1, count - fixed)
        return jnp.zeros((count,), jnp.int32).at[sequence[jnp.where(places < fixed, places, moved)]].set(jnp.asarray(lengths, jnp.int32))

    lengths = jnp.where(number % 4 == 0, named(heavy_load, number // 4), named(ordinary, number - number // 4 - 1))
    mixed = jax.random.permutation(jax.random.fold_in(own, 3), count)
    giver, receiver = mixed[0:count // 2 * 2:2], mixed[1:count // 2 * 2:2]
    margin = jnp.minimum(lengths[giver] - 1, reach - lengths[receiver]) // 2
    margin = jnp.where((giver == sequence[0]) | (receiver == sequence[0]) | (lengths[receiver] == 0), 0, jnp.maximum(margin, 0))
    moved = jax.random.randint(jax.random.fold_in(own, 4), (count // 2,), 0, 1 << 20) % (margin + 1)
    lengths = lengths.at[giver].add(-moved).at[receiver].add(moved)
    labels = jnp.searchsorted(jnp.cumsum(lengths), jnp.arange(rows * top), side="right").astype(jnp.int32)
    listing = labels.reshape(top, rows).T
    listing = listing[jax.random.permutation(jax.random.fold_in(own, 1), rows)]
    offset_by = jax.random.randint(jax.random.fold_in(own, 2), (rows, 1), 0, top)
    return jnp.take_along_axis(listing, (jnp.arange(top)[None, :] + offset_by) % top, axis=1)


def portions_of(number_of, total, bound, slope, full):
    weights = [(1 << 20) // math.isqrt(standing ** slope) + 1 for standing in range(1, number_of + 1)]
    largest = bound if full else min(bound, max(-(-total // number_of), total * weights[0] // sum(weights)))
    least = 1 if total - largest >= number_of - 1 else 0
    given, rest = [largest] + [least] * (number_of - 1), total - largest - least * (number_of - 1)
    while rest > 0:
        candidates = [i for i in range(1, number_of) if given[i] < largest] or [i for i in range(1, number_of) if given[i] < bound]
        mass, left = sum([weights[i] for i in candidates]), rest
        for i in candidates:
            extra = min(bound - given[i], max(1, left * weights[i] // mass), rest)
            given[i] = given[i] + extra
            rest = rest - extra
    return np.array(given)


def bell_draw(rng, shape, scale, most, cuts=(), kind=jnp.bfloat16):
    entries = jax.random.normal(rng, shape, jnp.float32) * scale
    if len(cuts) > 0:
        entries = shard_levels(rng, shape, cuts, -0.22, 0.18) * entries
    return jnp.clip(entries, min=-most, max=most).astype(kind)


def bell_draw_with(stream_key, shape, width, bound, cuts, heavy, kind=jnp.bfloat16):
    values = width * jax.random.normal(stream_key, shape, jnp.float32)
    if cuts:
        values = values * shard_levels(stream_key, shape, cuts, -0.22, 0.18)
    return jnp.clip(spiked(values, jax.random.fold_in(stream_key, 3), *heavy), -bound, bound).astype(kind)


def setup_inputs(seed: int = 0) -> dict:
    splits = jax.random.split(jax.random.key(seed), 10)
    patches = bell_draw(splits[0], (N_DP * SLOTS * BLK, D), 1.0, 6.0, ((0, 64),))
    live_blocks = draw_live_blocks(jax.random.fold_in(splits[9], 71), 0)
    owner_map_keys = jax.random.split(jax.random.fold_in(splits[2], 1), (N_DP * MERGED) // MERGED)
    owner_map_turns = jax.random.permutation(jax.random.fold_in(splits[2], 3), (N_DP * MERGED) // MERGED)
    owner_map = jax.vmap(lambda own, number: routed_block(jax.random.fold_in(splits[2], 2), own, number, MERGED, N_DP, 1, CAP_OWN, 0))(owner_map_keys, owner_map_turns).reshape((N_DP * MERGED, 1))
    vit_gain = jnp.clip(1.0 + 0.18 * jax.random.normal(splits[3], (D,), jnp.float32), 0.1, 1.9)
    fc1_weight = bell_draw(splits[4], (D, FF), D ** -0.5, 0.15625, ((1, 16),))
    fc2_weight = bell_draw(splits[5], (FF, D), FF ** -0.5, 0.078125, ((0, 16),))
    merge_gain = jnp.clip(1.0 + 0.18 * jax.random.normal(splits[6], (D,), jnp.float32), 0.1, 1.9)
    mid_weight = bell_draw(splits[7], (4 * D, 4 * D), (4 * D) ** -0.5, 0.078125, ((1, 16),))
    proj_weight = bell_draw_with(splits[8], (4 * D, EMB), (4 * D) ** -0.5, 0.125, ((0, 16),), (0, 1, 16, 2.0))
    return dict(patches=patches, live_blocks=live_blocks, owner_map=owner_map, vit_gain=vit_gain, fc1_weight=fc1_weight, fc2_weight=fc2_weight, merge_gain=merge_gain, mid_weight=mid_weight, proj_weight=proj_weight)


def layer_norm(values, gain):
    mean = lax.optimization_barrier(jnp.mean(values, axis=-1, keepdims=True))
    centered = values - mean
    variance = lax.optimization_barrier(jnp.mean(centered * centered, axis=-1, keepdims=True))
    return centered * lax.rsqrt(variance + 1e-06) * gain

def reference(patches, live_blocks, owner_map, vit_gain, fc1_weight, fc2_weight, merge_gain, mid_weight, proj_weight):
    blocks = patches.reshape(N_DP * SLOTS, BLK, D)
    flags = (jnp.arange(SLOTS, dtype=jnp.int32)[None, :] < live_blocks[:, None]).reshape(-1)

    def compute(rows):
        normed = layer_norm(rows.astype(jnp.float32), vit_gain).astype(jnp.bfloat16)
        up_vals = jnp.dot(normed, fc1_weight, preferred_element_type=jnp.float32)
        hidden = (up_vals * jax.nn.sigmoid(1.702 * up_vals)).astype(jnp.bfloat16)
        vit_out = (rows.astype(jnp.float32) + jnp.dot(hidden, fc2_weight, preferred_element_type=jnp.float32)).astype(jnp.bfloat16)
        merged = layer_norm(vit_out.astype(jnp.float32), merge_gain).astype(jnp.bfloat16).reshape(BLK // 4, 4 * D)
        middle = jnp.dot(merged, mid_weight, preferred_element_type=jnp.float32)
        middle = jax.nn.gelu(middle, approximate=False).astype(jnp.bfloat16)
        return jnp.dot(middle, proj_weight, preferred_element_type=jnp.float32).astype(jnp.bfloat16)

    def vacant(rows):
        return jnp.zeros((BLK // 4, EMB), jnp.bfloat16)

    def one_block(items):
        rows, flag = items
        return lax.cond(flag, compute, vacant, rows)
    projected = lax.map(one_block, (blocks, flags)).reshape(N_DP * MERGED, EMB)
    owners = owner_map[:, 0].reshape(N_DP, MERGED)
    index = jnp.arange(MERGED, dtype=jnp.int32)
    same = (owners[:, :, None] == owners[:, None, :]) & (index[None, None, :] < index[None, :, None])
    slot = lax.optimization_barrier(jnp.sum(same.astype(jnp.int32), axis=-1)).astype(jnp.int32)
    ranks = jnp.arange(N_DP, dtype=jnp.int32)[:, None]
    dest = (owners * (N_DP * CAP_OWN) + ranks * CAP_OWN + slot).astype(jnp.int32)
    result = jnp.zeros((N_DP * N_DP * CAP_OWN, EMB), jnp.bfloat16)
    return result.at[dest.reshape(-1)].set(projected)
```

```python
import jax
import jax.numpy as jnp
from jax import lax
from jax.experimental import pallas as pl
from jax.experimental.pallas import tpu as pltpu
from jax.sharding import PartitionSpec as P

MESH = pl.DeviceIdType.MESH
F32 = jnp.float32
BF16 = jnp.bfloat16
STAGES = 2
SIGNS = (1, -1)


def dot(a, b):
    return jnp.dot(a, b, preferred_element_type=F32)


def layer_norm(values, gain):
    mean = jnp.mean(values, axis=-1, keepdims=True)
    centered = values - mean
    variance = jnp.mean(centered * centered, axis=-1, keepdims=True)
    return centered * lax.rsqrt(variance + 1e-06) * gain


class Reduce:
    def __init__(self, me, ring, own, rounded, relay, got_far, got_near, send_sem, recv_sem):
        self.me, self.ring = me, ring
        self.own, self.rounded, self.relay = own, rounded, relay
        self.got_far, self.got_near = got_far, got_near
        self.send_sem, self.recv_sem = send_sem, recv_sem

    def place(self, steps):
        return lax.rem(self.me + (steps + self.ring), self.ring)

    def far(self, d, k, source=None):
        source = self.relay.at[d, k] if source is None else source
        return pltpu.make_async_remote_copy(
            src_ref=source, dst_ref=self.got_far.at[d, k],
            send_sem=self.send_sem.at[d, k, 0], recv_sem=self.recv_sem.at[d, k, 0],
            device_id={"tensor": self.place(2 * SIGNS[d])}, device_id_type=MESH)

    def near(self, d, k):
        return pltpu.make_async_remote_copy(
            src_ref=self.rounded.at[self.place((7 - 2 * k) * SIGNS[d])], dst_ref=self.got_near.at[d, k],
            send_sem=self.send_sem.at[d, k, 1], recv_sem=self.recv_sem.at[d, k, 1],
            device_id={"tensor": self.place(SIGNS[d])}, device_id_type=MESH)

    def first(self):
        self.far(0, 0, self.rounded.at[self.place(8)]).start()
        for d in (0, 1):
            self.near(d, 0).start()
        for d in (0, 1):
            self.near(d, 1).start()

    def arrived(self, d, k):
        if not (d == 1 and k == 0):
            self.far(d, k).wait_recv()
        self.near(d, k).wait_recv()
        total = self.got_near[d, k].astype(F32)
        if not (d == 1 and k == 0):
            total = total + self.got_far[d, k].astype(F32)
        return total

    def step(self, k):
        for d in (0, 1):
            got = self.arrived(d, k - 1)
            mine = self.own[self.place((8 - 2 * k) * SIGNS[d])]
            self.relay[d, k] = (mine + got).astype(BF16)
            self.far(d, k).start()
            if k < 3:
                self.near(d, k + 1).start()

    def last(self):
        return self.own[self.me] + self.arrived(0, 3) + self.arrived(1, 3)

    def drain(self):
        for d in (0, 1):
            for k in range(4):
                if not (d == 1 and k == 0):
                    self.far(d, k).wait_send()
                self.near(d, k).wait_send()


class Gather:
    def __init__(self, me, ring, chunks, send_sem, recv_sem):
        self.me, self.ring, self.chunks = me, ring, chunks
        self.send_sem, self.recv_sem = send_sem, recv_sem

    def place(self, steps):
        return lax.rem(self.me + (steps + self.ring), self.ring)

    def copy(self, d, k, near):
        chunk = self.chunks.at[self.place(-2 * k * SIGNS[d])]
        return pltpu.make_async_remote_copy(
            src_ref=chunk, dst_ref=chunk,
            send_sem=self.send_sem.at[d, k, near], recv_sem=self.recv_sem.at[d, k, near],
            device_id={"tensor": self.place((2 - near) * SIGNS[d])}, device_id_type=MESH)

    def landing(self, d, k, near):
        chunk = self.chunks.at[self.place((-2 * (k + 1) + near) * SIGNS[d])]
        return pltpu.make_async_remote_copy(
            src_ref=chunk, dst_ref=chunk,
            send_sem=self.send_sem.at[d, k, near], recv_sem=self.recv_sem.at[d, k, near],
            device_id={"tensor": self.place((2 - near) * SIGNS[d])}, device_id_type=MESH)

    def step(self, k):
        for d in (0, 1):
            if k > 0:
                self.landing(d, k - 1, 0).wait_recv()
            if not (d == 1 and k == 3):
                self.copy(d, k, 0).start()
        for d in (0, 1):
            self.copy(d, k, 1).start()

    def last(self):
        self.landing(0, 3, 0).wait_recv()
        for d in (0, 1):
            for k in range(4):
                self.landing(d, k, 1).wait_recv()

    def drain(self):
        for d in (0, 1):
            for k in range(4):
                if not (d == 1 and k == 3):
                    self.copy(d, k, 0).wait_send()
                self.copy(d, k, 1).wait_send()


def kernel(
    live_ref, owner_ref, vit_gain_ref, merge_gain_ref, patches_ref, fc1_ref, fc2_ref, mid_hbm, proj_hbm,
    out_ref,
    mid_w, proj_w, rows, own1, round1, relay1, far1, near1, chunks, own2, round2, relay2, far2, near2,
    outgoing, incoming,
    weight_sem, send1, recv1, send_g, recv_g, send2, recv2, send_x, recv_x,
):
    ring = lax.axis_size("tensor")
    ndp = lax.axis_size("dp")
    me = lax.axis_index("tensor")
    here = lax.axis_index("dp")
    merged = patches_ref.shape[0] // 4
    count = merged // STAGES
    width = patches_ref.shape[1]

    load_mid = pltpu.make_async_copy(mid_hbm, mid_w, weight_sem.at[0])
    load_proj = pltpu.make_async_copy(proj_hbm, proj_w, weight_sem.at[1])
    load_mid.start()
    load_proj.start()

    barrier = pltpu.get_barrier_semaphore()
    for hops in (1, 2, ring - 2, ring - 1):
        pl.semaphore_signal(barrier, inc=1, device_id={"tensor": lax.rem(me + hops, ring)}, device_id_type=MESH)

    def greet(hops, carry):
        pl.semaphore_signal(barrier, inc=1, device_id={"dp": lax.rem(here + hops, ndp)}, device_id_type=MESH)
        return carry

    lax.fori_loop(1, ndp, greet, 0)

    def mlp(s):
        total = 4 * count
        to = lax.broadcasted_iota(jnp.int32, (total, total), 0)
        source = lax.broadcasted_iota(jnp.int32, (total, total), 1)
        order = (source == 4 * (to % count) + to // count).astype(BF16)
        ordered = dot(order, patches_ref[s * total : (s + 1) * total, :])
        rows[s] = ordered.astype(BF16).reshape(rows.shape[1:])
        normed = layer_norm(ordered, vit_gain_ref[...]).astype(BF16)
        up = dot(normed, fc1_ref[...])
        hidden = (up * jax.nn.sigmoid(1.702 * up)).astype(BF16)
        partial = dot(hidden, fc2_ref[...]).reshape(rows.shape[1:])
        own1[s] = partial
        round1[s] = partial.astype(BF16)

    stages = range(STAGES)
    sums1 = [
        Reduce(me, ring, own1.at[s], round1.at[s], relay1.at[s], far1.at[s], near1.at[s], send1.at[s], recv1.at[s])
        for s in stages
    ]
    gathers = [Gather(me, ring, chunks.at[s], send_g.at[s], recv_g.at[s]) for s in stages]
    sums2 = [
        Reduce(me, ring, own2.at[s], round2.at[s], relay2.at[s], far2.at[s], near2.at[s], send2.at[s], recv2.at[s])
        for s in stages
    ]

    for s in stages:
        mlp(s)
        if s == 0:
            pl.semaphore_wait(barrier, 4 + ndp - 1)
        sums1[s].first()
    for k in (1, 2, 3):
        for s in stages:
            sums1[s].step(k)
    for s in stages:
        vit_out = (rows[s, me].astype(F32) + sums1[s].last()).astype(BF16)
        chunks[s, me] = layer_norm(vit_out.astype(F32), merge_gain_ref[...]).astype(BF16)
        gathers[s].step(0)
    for k in (1, 2, 3):
        for s in stages:
            gathers[s].step(k)
    load_mid.wait()
    load_proj.wait()
    emb = own2.shape[3]
    for s in stages:
        gathers[s].last()
        middle = jnp.zeros((count, mid_w.shape[1]), F32)
        part = ring // 4
        for j in range(4):
            block = chunks[s, part * j : part * (j + 1)].reshape(count, width)
            middle = middle + dot(block, mid_w[j * width : (j + 1) * width, :])
        middle = (0.5 * middle * (1.0 + lax.erf(middle * 0.7071067811865476))).astype(BF16)
        for t in range(ring):
            term = dot(middle, proj_w[:, t * emb : (t + 1) * emb])
            own2[s, t] = term
            round2[s, t] = term.astype(BF16)
        sums2[s].first()
    for k in (1, 2, 3):
        for s in stages:
            sums2[s].step(k)

    owner = jnp.broadcast_to(owner_ref[...].astype(F32), (merged, merged)).T.astype(jnp.int32)
    across = lax.broadcasted_iota(jnp.int32, (merged, merged), 1)
    down = lax.broadcasted_iota(jnp.int32, (merged, merged), 0)
    own_col = jnp.broadcast_to(owner_ref[...], (merged, merged))
    slot = jnp.sum(jnp.where((owner == own_col) & (down < across), 1.0, 0.0), axis=0, keepdims=True)
    column = lax.broadcasted_iota(jnp.int32, (ndp, merged), 1)
    target = lax.broadcasted_iota(jnp.int32, (ndp, merged), 0)
    kept = (owner[:1] == target) & (column * 4 // (4 * merged // 4) < live_ref[0])
    placing = [jnp.where(kept & (slot == float(k)), 1.0, 0.0).astype(BF16) for k in (0, 1)]

    final = jnp.concatenate([sums2[s].last().astype(BF16) for s in stages], axis=0)
    lanes = outgoing.shape[2]
    for k in (0, 1):
        placed = dot(placing[k], final)
        for h in range(emb // lanes):
            outgoing[:, 2 * k + h, :] = placed[:, h * lanes : (h + 1) * lanes]

    def send(hops, carry):
        peer = lax.rem(here + hops, ndp)
        pltpu.make_async_remote_copy(
            src_ref=outgoing.at[peer], dst_ref=incoming.at[here], send_sem=send_x, recv_sem=recv_x,
            device_id={"dp": peer}, device_id_type=MESH).start()
        return carry

    lax.fori_loop(1, ndp, send, 0)
    incoming[here] = outgoing[here]
    for s in stages:
        sums1[s].drain()
        gathers[s].drain()
        sums2[s].drain()
    others = pl.ds(0, ndp - 1)
    pltpu.make_async_copy(outgoing.at[others], incoming.at[others], send_x).wait()
    pltpu.make_async_copy(outgoing.at[others], incoming.at[others], recv_x).wait()

    row = lax.broadcasted_iota(jnp.int32, (2 * ndp, ndp), 0)
    origin = lax.broadcasted_iota(jnp.int32, (2 * ndp, ndp), 1)
    result = jnp.zeros((2 * ndp, emb), F32)
    for k in (0, 1):
        part = jnp.concatenate([incoming[:, 2 * k + h, :] for h in range(emb // lanes)], axis=1).astype(BF16)
        result = result + dot((row == 2 * origin + k).astype(BF16), part)
    out_ref[...] = result.astype(BF16)


def solution(mesh):
    ring, ndp = mesh.shape["tensor"], mesh.shape["dp"]

    def body(patches, live, owners, vit_gain, fc1, fc2, merge_gain, mid, proj):
        total, width = patches.shape
        chunk = total // STAGES // ring
        count = total // 4 // STAGES
        emb = proj.shape[1] // ring
        vmem = pl.BlockSpec(memory_space=pltpu.VMEM)
        return pl.pallas_call(
            kernel,
            out_shape=jax.ShapeDtypeStruct((2 * ndp, emb), BF16),
            in_specs=[pl.BlockSpec(memory_space=pltpu.SMEM)] + [vmem] * 6 + [pl.BlockSpec(memory_space=pl.ANY)] * 2,
            out_specs=vmem,
            scratch_shapes=[
                pltpu.VMEM(mid.shape, BF16),
                pltpu.VMEM(proj.shape, BF16),
                pltpu.VMEM((STAGES, ring, chunk, width), BF16),
                pltpu.VMEM((STAGES, ring, chunk, width), F32),
                pltpu.VMEM((STAGES, ring, chunk, width), BF16),
                pltpu.VMEM((STAGES, 2, 4, chunk, width), BF16),
                pltpu.VMEM((STAGES, 2, 4, chunk, width), BF16),
                pltpu.VMEM((STAGES, 2, 4, chunk, width), BF16),
                pltpu.VMEM((STAGES, ring, chunk, width), BF16),
                pltpu.VMEM((STAGES, ring, count, emb), F32),
                pltpu.VMEM((STAGES, ring, count, emb), BF16),
                pltpu.VMEM((STAGES, 2, 4, count, emb), BF16),
                pltpu.VMEM((STAGES, 2, 4, count, emb), BF16),
                pltpu.VMEM((STAGES, 2, 4, count, emb), BF16),
                pltpu.VMEM((ndp, 2 * emb // 128, 128), F32),
                pltpu.VMEM((ndp, 2 * emb // 128, 128), F32),
                pltpu.SemaphoreType.DMA((2,)),
            ]
            + [pltpu.SemaphoreType.DMA((STAGES, 2, 4, 2))] * 6
            + [pltpu.SemaphoreType.DMA, pltpu.SemaphoreType.DMA],
            compiler_params=pltpu.CompilerParams(
                collective_id=0, has_side_effects=True, vmem_limit_bytes=56 * 2**20
            ),
            name="vision_block",
        )(live, owners, vit_gain.reshape(1, width), merge_gain.reshape(1, width), patches, fc1, fc2, mid, proj)

    return jax.shard_map(
        body,
        mesh=mesh,
        in_specs=(
            P("dp", None), P("dp"), P("dp", None), P(), P(None, "tensor"), P("tensor", None), P(),
            P(None, "tensor"), P("tensor", None),
        ),
        out_specs=P("dp", "tensor"),
        check_vma=False,
    )
```

```python
import jax
import jax.numpy as jnp
from jax import lax
from jax.experimental import pallas as pl
from jax.experimental.pallas import tpu as pltpu
from jax.sharding import PartitionSpec as P

MESH = pl.DeviceIdType.MESH
F32 = jnp.float32
BF16 = jnp.bfloat16
STAGES = 2
HALVES = 2
SIGNS = (1, -1)


def dot(a, b):
    return jnp.dot(a, b, preferred_element_type=F32)


def dot_t(a, b):
    return lax.dot_general(a, b, (((1,), (1,)), ((), ())), preferred_element_type=F32)


def layer_norm(values, gain):
    mean = jnp.mean(values, axis=-1, keepdims=True)
    centered = values - mean
    variance = jnp.mean(centered * centered, axis=-1, keepdims=True)
    return centered * lax.rsqrt(variance + 1e-06) * gain


class Reduce:
    def __init__(self, me, ring, longer, own, rounded, relay, got_far, got_near, send_sem, recv_sem):
        self.me, self.ring, self.longer = me, ring, longer
        self.own, self.rounded, self.relay = own, rounded, relay
        self.got_far, self.got_near = got_far, got_near
        self.send_sem, self.recv_sem = send_sem, recv_sem

    def place(self, steps):
        return lax.rem(self.me + (steps + self.ring), self.ring)

    def far(self, d, k, source=None):
        source = self.relay.at[d, k] if source is None else source
        return pltpu.make_async_remote_copy(
            src_ref=source, dst_ref=self.got_far.at[d, k],
            send_sem=self.send_sem.at[d, k, 0], recv_sem=self.recv_sem.at[d, k, 0],
            device_id={"tensor": self.place(2 * SIGNS[d])}, device_id_type=MESH)

    def near(self, d, k):
        return pltpu.make_async_remote_copy(
            src_ref=self.rounded.at[self.place((7 - 2 * k) * SIGNS[d])], dst_ref=self.got_near.at[d, k],
            send_sem=self.send_sem.at[d, k, 1], recv_sem=self.recv_sem.at[d, k, 1],
            device_id={"tensor": self.place(SIGNS[d])}, device_id_type=MESH)

    def first(self):
        self.far(self.longer, 0, self.rounded.at[self.place(8)]).start()
        for d in (0, 1):
            self.near(d, 0).start()
        for d in (0, 1):
            self.near(d, 1).start()

    def arrived(self, d, k):
        if k > 0 or d == self.longer:
            self.far(d, k).wait_recv()
        self.near(d, k).wait_recv()
        total = self.got_near[d, k].astype(F32)
        if k > 0 or d == self.longer:
            total = total + self.got_far[d, k].astype(F32)
        return total

    def step(self, k):
        for d in (0, 1):
            got = self.arrived(d, k - 1)
            mine = self.own[self.place((8 - 2 * k) * SIGNS[d])]
            self.relay[d, k] = (mine + got).astype(BF16)
            self.far(d, k).start()
            if k < 3:
                self.near(d, k + 1).start()

    def last(self):
        return self.own[self.me] + self.arrived(0, 3) + self.arrived(1, 3)

    def drain(self):
        for d in (0, 1):
            for k in range(4):
                if k > 0 or d == self.longer:
                    self.far(d, k).wait_send()
                self.near(d, k).wait_send()


class Gather:
    def __init__(self, me, ring, longer, chunks, send_sem, recv_sem):
        self.me, self.ring, self.longer, self.chunks = me, ring, longer, chunks
        self.send_sem, self.recv_sem = send_sem, recv_sem

    def place(self, steps):
        return lax.rem(self.me + (steps + self.ring), self.ring)

    def copy(self, d, k, near):
        chunk = self.chunks.at[self.place(-2 * k * SIGNS[d])]
        return pltpu.make_async_remote_copy(
            src_ref=chunk, dst_ref=chunk,
            send_sem=self.send_sem.at[d, k, near], recv_sem=self.recv_sem.at[d, k, near],
            device_id={"tensor": self.place((2 - near) * SIGNS[d])}, device_id_type=MESH)

    def landing(self, d, k, near):
        chunk = self.chunks.at[self.place((-2 * (k + 1) + near) * SIGNS[d])]
        return pltpu.make_async_remote_copy(
            src_ref=chunk, dst_ref=chunk,
            send_sem=self.send_sem.at[d, k, near], recv_sem=self.recv_sem.at[d, k, near],
            device_id={"tensor": self.place((2 - near) * SIGNS[d])}, device_id_type=MESH)

    def step(self, k):
        for d in (0, 1):
            if k > 0:
                self.landing(d, k - 1, 0).wait_recv()
            if k < 3 or d == self.longer:
                self.copy(d, k, 0).start()
        for d in (0, 1):
            self.copy(d, k, 1).start()

    def last(self):
        self.landing(self.longer, 3, 0).wait_recv()
        for d in (0, 1):
            for k in range(4):
                self.landing(d, k, 1).wait_recv()

    def drain(self):
        for d in (0, 1):
            for k in range(4):
                if k < 3 or d == self.longer:
                    self.copy(d, k, 0).wait_send()
                self.copy(d, k, 1).wait_send()


def kernel(
    live_ref, owner_ref, vit_gain_ref, merge_gain_ref, patches_hbm, fc1_hbm, fc2_hbm, mid_hbm, proj_hbm,
    out_ref,
    patches_ref, fc1_ref, fc2_ref, mid_w, proj_w,
    rows, own1, round1, relay1, far1, near1, chunks, own2, round2, relay2, far2, near2,
    outgoing, incoming,
    load_sem, send1, recv1, send_g, recv_g, send2, recv2, send_x, recv_x,
):
    ring = lax.axis_size("tensor")
    ndp = lax.axis_size("dp")
    me = lax.axis_index("tensor")
    here = lax.axis_index("dp")
    merged = patches_ref.shape[0] // 4
    count = merged // STAGES
    width = patches_ref.shape[1]
    part = width // HALVES
    emb = own2.shape[4]

    barrier = pltpu.get_barrier_semaphore()
    for hops in (1, 2, ring - 2, ring - 1):
        pl.semaphore_signal(barrier, inc=1, device_id={"tensor": lax.rem(me + hops, ring)}, device_id_type=MESH)
    loads = [
        pltpu.make_async_copy(source, target, load_sem.at[i])
        for i, (source, target) in enumerate((
            (patches_hbm, patches_ref), (fc1_hbm, fc1_ref), (fc2_hbm, fc2_ref), (mid_hbm, mid_w), (proj_hbm, proj_w)))
    ]
    for load in loads:
        load.start()

    def greet(hops, carry):
        pl.semaphore_signal(barrier, inc=1, device_id={"dp": lax.rem(here + hops, ndp)}, device_id_type=MESH)
        return carry

    lax.fori_loop(1, ndp, greet, 0)

    def mlp(s):
        total = 4 * count
        to = lax.broadcasted_iota(jnp.int32, (total, total), 0)
        source = lax.broadcasted_iota(jnp.int32, (total, total), 1)
        order = (source == 4 * (to % count) + to // count).astype(BF16)
        ordered = dot(order, patches_ref[s * total : (s + 1) * total, :])
        rows[s] = ordered.astype(BF16).reshape(rows.shape[1:])
        normed = layer_norm(ordered, vit_gain_ref[...].reshape(1, width)).astype(BF16)
        up = dot_t(normed, fc1_ref[...])
        hidden = (up * jax.nn.sigmoid(1.702 * up)).astype(BF16)
        for h in range(HALVES):
            partial = dot(hidden, fc2_ref[:, h * part : (h + 1) * part]).reshape(own1.shape[2:])
            own1[s, h] = partial
            round1[s, h] = partial.astype(BF16)

    stages, halves = range(STAGES), range(HALVES)
    chains = [(s, h) for s in stages for h in halves]
    sums1 = {
        c: Reduce(me, ring, c[1], own1.at[c], round1.at[c], relay1.at[c], far1.at[c], near1.at[c], send1.at[c], recv1.at[c])
        for c in chains
    }
    gathers = {c: Gather(me, ring, c[1], chunks.at[c], send_g.at[c], recv_g.at[c]) for c in chains}
    sums2 = {
        c: Reduce(me, ring, c[1], own2.at[c], round2.at[c], relay2.at[c], far2.at[c], near2.at[c], send2.at[c], recv2.at[c])
        for c in chains
    }

    for load in loads[:3]:
        load.wait()
    for s in stages:
        mlp(s)
        if s == 0:
            pl.semaphore_wait(barrier, 4 + ndp - 1)
        for h in halves:
            sums1[s, h].first()
    for k in (1, 2, 3):
        for c in chains:
            sums1[c].step(k)
    for s in stages:
        summed = jnp.concatenate([sums1[s, h].last() for h in halves], axis=1)
        vit_out = (rows[s, me].astype(F32) + summed).astype(BF16)
        normed = layer_norm(vit_out.astype(F32), merge_gain_ref[...].reshape(1, width)).astype(BF16)
        for h in halves:
            chunks[s, h, me] = normed[:, h * part : (h + 1) * part]
            gathers[s, h].step(0)
    for k in (1, 2, 3):
        for c in chains:
            gathers[c].step(k)
    for load in loads[3:]:
        load.wait()
    quarter = ring // 4
    for s in stages:
        middle = jnp.zeros((count, mid_w.shape[0]), F32)
        for h in halves:
            gathers[s, h].last()
            for j in range(4):
                block = chunks[s, h, quarter * j : quarter * (j + 1)].reshape(count, part)
                first = j * width + h * part
                middle = middle + dot_t(block, mid_w[:, first : first + part])
        middle = (0.5 * middle * (1.0 + lax.erf(middle * 0.7071067811865476))).astype(BF16)
        for t in range(ring):
            term = dot(middle, proj_w[:, t * emb : (t + 1) * emb])
            for h in halves:
                piece = term[h * (count // HALVES) : (h + 1) * (count // HALVES)]
                own2[s, h, t] = piece
                round2[s, h, t] = piece.astype(BF16)
        for h in halves:
            sums2[s, h].first()
    for k in (1, 2, 3):
        for c in chains:
            sums2[c].step(k)

    owner = jnp.broadcast_to(owner_ref[...], (merged, merged))
    across = lax.broadcasted_iota(jnp.int32, (merged, merged), 1)
    down = lax.broadcasted_iota(jnp.int32, (merged, merged), 0)
    own_col = owner.astype(F32).T.astype(jnp.int32)
    slot = jnp.sum(jnp.where((owner == own_col) & (down < across), 1.0, 0.0), axis=0, keepdims=True)
    column = lax.broadcasted_iota(jnp.int32, (ndp, merged), 1)
    target = lax.broadcasted_iota(jnp.int32, (ndp, merged), 0)
    kept = (owner[:1] == target) & (column * 4 // (4 * merged // 4) < live_ref[0])
    placing = [jnp.where(kept & (slot == float(k)), 1.0, 0.0).astype(BF16) for k in (0, 1)]

    final = jnp.concatenate([sums2[c].last().astype(BF16) for c in chains], axis=0)
    lanes = outgoing.shape[2]
    for k in (0, 1):
        placed = dot(placing[k], final)
        for h in range(emb // lanes):
            outgoing[:, 2 * k + h, :] = placed[:, h * lanes : (h + 1) * lanes]

    def send(hops, carry):
        peer = lax.rem(here + hops, ndp)
        pltpu.make_async_remote_copy(
            src_ref=outgoing.at[peer], dst_ref=incoming.at[here], send_sem=send_x, recv_sem=recv_x,
            device_id={"dp": peer}, device_id_type=MESH).start()
        return carry

    lax.fori_loop(1, ndp, send, 0)
    incoming[here] = outgoing[here]
    for c in chains:
        sums1[c].drain()
        gathers[c].drain()
        sums2[c].drain()
    others = pl.ds(0, ndp - 1)
    pltpu.make_async_copy(outgoing.at[others], incoming.at[others], send_x).wait()
    pltpu.make_async_copy(outgoing.at[others], incoming.at[others], recv_x).wait()

    row = lax.broadcasted_iota(jnp.int32, (2 * ndp, ndp), 0)
    origin = lax.broadcasted_iota(jnp.int32, (2 * ndp, ndp), 1)
    result = jnp.zeros((2 * ndp, emb), F32)
    for k in (0, 1):
        part = jnp.concatenate([incoming[:, 2 * k + h, :] for h in range(emb // lanes)], axis=1).astype(BF16)
        result = result + dot((row == 2 * origin + k).astype(BF16), part)
    out_ref[...] = result.astype(BF16)


def solution(mesh):
    ring, ndp = mesh.shape["tensor"], mesh.shape["dp"]

    def body(patches, live, owners, vit_gain, fc1, fc2, merge_gain, mid, proj):
        total, width = patches.shape
        chunk = total // STAGES // ring
        count = total // 4 // STAGES
        emb = proj.shape[1] // ring
        vmem = pl.BlockSpec(memory_space=pltpu.VMEM)
        part, rows = width // HALVES, count // HALVES
        lead = (STAGES, HALVES)
        return pl.pallas_call(
            kernel,
            out_shape=jax.ShapeDtypeStruct((2 * ndp, emb), BF16),
            in_specs=[pl.BlockSpec(memory_space=pltpu.SMEM)] + [vmem] * 3 + [pl.BlockSpec(memory_space=pl.ANY)] * 5,
            out_specs=vmem,
            scratch_shapes=[
                pltpu.VMEM(patches.shape, BF16),
                pltpu.VMEM(fc1.shape[::-1], BF16),
                pltpu.VMEM(fc2.shape, BF16),
                pltpu.VMEM(mid.shape[::-1], BF16),
                pltpu.VMEM(proj.shape, BF16),
                pltpu.VMEM((STAGES, ring, chunk, width), BF16),
                pltpu.VMEM(lead + (ring, chunk, part), F32),
                pltpu.VMEM(lead + (ring, chunk, part), BF16),
                pltpu.VMEM(lead + (2, 4, chunk, part), BF16),
                pltpu.VMEM(lead + (2, 4, chunk, part), BF16),
                pltpu.VMEM(lead + (2, 4, chunk, part), BF16),
                pltpu.VMEM(lead + (ring, chunk, part), BF16),
                pltpu.VMEM(lead + (ring, rows, emb), F32),
                pltpu.VMEM(lead + (ring, rows, emb), BF16),
                pltpu.VMEM(lead + (2, 4, rows, emb), BF16),
                pltpu.VMEM(lead + (2, 4, rows, emb), BF16),
                pltpu.VMEM(lead + (2, 4, rows, emb), BF16),
                pltpu.VMEM((ndp, 2 * emb // 128, 128), F32),
                pltpu.VMEM((ndp, 2 * emb // 128, 128), F32),
                pltpu.SemaphoreType.DMA((5,)),
            ]
            + [pltpu.SemaphoreType.DMA(lead + (2, 4, 2))] * 6
            + [pltpu.SemaphoreType.DMA, pltpu.SemaphoreType.DMA],
            compiler_params=pltpu.CompilerParams(
                collective_id=0, has_side_effects=True, vmem_limit_bytes=56 * 2**20
            ),
            name="vision_block",
        )(live, owners.reshape(1, total // 4), vit_gain, merge_gain, patches, fc1.T, fc2, mid.T, proj)

    return jax.shard_map(
        body,
        mesh=mesh,
        in_specs=(
            P("dp", None), P("dp"), P("dp", None), P(), P(None, "tensor"), P("tensor", None), P(),
            P(None, "tensor"), P("tensor", None),
        ),
        out_specs=P("dp", "tensor"),
        check_vma=False,
    )
```

```python
import jax
import jax.numpy as jnp
from jax import lax
from jax.experimental import pallas as pl
from jax.experimental.pallas import tpu as pltpu
from jax.sharding import PartitionSpec as P

MESH = pl.DeviceIdType.MESH
F32 = jnp.float32
BF16 = jnp.bfloat16
STAGES = 2
HALVES = 2
SIGNS = (1, -1)
SUM1 = ((2, 2, 2, 2), (1, 2, 2, 2))
GATHER = ((2, 2, 2, 2), (2, 2, 2, 1))
SUM2 = ((2, 2, 2, 2), (1, 2, 2, 2))
DEPTH = 4


def dot(a, b):
    return jnp.dot(a, b, preferred_element_type=F32)


def dot_t(a, b):
    return lax.dot_general(a, b, (((1,), (1,)), ((), ())), preferred_element_type=F32)


def layer_norm(values, gain):
    mean = jnp.mean(values, axis=-1, keepdims=True)
    centered = values - mean
    variance = jnp.mean(centered * centered, axis=-1, keepdims=True)
    return centered * lax.rsqrt(variance + 1e-06) * gain


def positions(hops):
    left, places = sum(hops), []
    for hop in hops:
        places.append(left)
        left -= hop
    return places


class Reduce:
    def __init__(self, me, ring, sides, own, rounded, relay, got, send_sem, recv_sem):
        self.me, self.ring, self.sides = me, ring, sides
        self.places = [positions(hops) for hops in sides]
        self.own, self.rounded, self.relay = own, rounded, relay
        self.got = got
        self.send_sem, self.recv_sem = send_sem, recv_sem
        self.steps = max(len(hops) for hops in sides)

    def place(self, steps):
        return lax.rem(self.me + (steps + self.ring), self.ring)

    def far(self, d, k):
        source = self.relay.at[d, k] if k else self.rounded.at[self.place(self.places[d][0] * SIGNS[d])]
        return pltpu.make_async_remote_copy(
            src_ref=source, dst_ref=self.got.at[d, k, 0],
            send_sem=self.send_sem, recv_sem=self.recv_sem.at[d, k],
            device_id={"tensor": self.place(self.sides[d][k] * SIGNS[d])}, device_id_type=MESH)

    def has_near(self, d, k):
        return k < len(self.sides[d]) and self.sides[d][k] == 2

    def near(self, d, k):
        return pltpu.make_async_remote_copy(
            src_ref=self.rounded.at[self.place((self.places[d][k] - 1) * SIGNS[d])], dst_ref=self.got.at[d, k, 1],
            send_sem=self.send_sem, recv_sem=self.recv_sem.at[d, k],
            device_id={"tensor": self.place(SIGNS[d])}, device_id_type=MESH)

    def first(self):
        for d in (0, 1):
            self.far(d, 0).start()
        for k in (0, 1):
            for d in (0, 1):
                if self.has_near(d, k):
                    self.near(d, k).start()

    def arrived(self, d, k):
        if not self.has_near(d, k):
            self.far(d, k).wait_recv()
            return self.got[d, k, 0].astype(F32)
        both = self.got.at[d, k]
        pltpu.make_async_copy(both, both, self.recv_sem.at[d, k]).wait()
        return self.got[d, k, 0].astype(F32) + self.got[d, k, 1].astype(F32)

    def step(self, k):
        for d in (0, 1):
            if k < len(self.sides[d]):
                got = self.arrived(d, k - 1)
                mine = self.own[self.place(self.places[d][k] * SIGNS[d])]
                self.relay[d, k] = (mine + got).astype(BF16)
                self.far(d, k).start()
                if self.has_near(d, k + 1):
                    self.near(d, k + 1).start()

    def last(self):
        return self.own[self.me] + self.arrived(0, len(self.sides[0]) - 1) + self.arrived(1, len(self.sides[1]) - 1)

    def drain(self):
        every = self.rounded.at[pl.ds(0, self.ring - 1)]
        pltpu.make_async_copy(every, every, self.send_sem).wait()


class Gather:
    def __init__(self, me, ring, sides, chunks, send_sem, recv_sem, near_sem):
        self.me, self.ring, self.sides, self.chunks = me, ring, sides, chunks
        self.send_sem, self.recv_sem, self.near_sem = send_sem, recv_sem, near_sem
        self.steps = max(len(hops) for hops in sides)

    def place(self, steps):
        return lax.rem(self.me + (steps + self.ring), self.ring)

    def copy(self, d, k, hop, distance):
        chunk = self.chunks.at[self.place(-distance * SIGNS[d])]
        return pltpu.make_async_remote_copy(
            src_ref=chunk, dst_ref=chunk, send_sem=self.send_sem,
            recv_sem=self.near_sem if hop < self.sides[d][k] else self.recv_sem.at[d, k],
            device_id={"tensor": self.place(hop * SIGNS[d])}, device_id_type=MESH)

    def sent(self, d, k, hop):
        return self.copy(d, k, hop, sum(self.sides[d][:k]))

    def landed(self, d, k, hop):
        return self.copy(d, k, hop, sum(self.sides[d][:k]) + hop)

    def step(self, k):
        live = [d for d in (0, 1) if k < len(self.sides[d])]
        for d in live:
            if k > 0:
                self.landed(d, k - 1, self.sides[d][k - 1]).wait_recv()
            self.sent(d, k, self.sides[d][k]).start()
        for d in live:
            if self.sides[d][k] == 2:
                self.sent(d, k, 1).start()

    def last(self):
        for d in (0, 1):
            k = len(self.sides[d]) - 1
            self.landed(d, k, self.sides[d][k]).wait_recv()
        between = self.chunks.at[pl.ds(0, sum(hops.count(2) for hops in self.sides))]
        pltpu.make_async_copy(between, between, self.near_sem).wait()

    def drain(self):
        every = self.chunks.at[pl.ds(0, self.ring - 1)]
        pltpu.make_async_copy(every, every, self.send_sem).wait()


def kernel(
    live_hbm, owner_hbm, vit_gain_hbm, merge_gain_hbm, patches_hbm, fc1_hbm, fc2_hbm, mid_hbm, proj_hbm,
    out_ref,
    live_ref, owner_ref, vit_gain_ref, merge_gain_ref, patches_ref, fc1_ref, fc2_ref, mid_w, proj_w,
    rows, own1, round1, relay1, got1, chunks, own2, round2, relay2, got2,
    outgoing, incoming,
    load_sem, send1, recv1, send_g, recv_g, near_g, send2, recv2, send_x, recv_x,
):
    ring = lax.axis_size("tensor")
    ndp = lax.axis_size("dp")
    me = lax.axis_index("tensor")
    here = lax.axis_index("dp")
    merged = patches_ref.shape[0] // 4
    count = merged // STAGES
    width = patches_ref.shape[1]
    part = width // HALVES
    emb = own2.shape[4]

    barrier = pltpu.get_barrier_semaphore()
    for hops in (1, 2, ring - 2, ring - 1):
        pl.semaphore_signal(barrier, inc=1, device_id={"tensor": lax.rem(me + hops, ring)}, device_id_type=MESH)
    loads = [
        pltpu.make_async_copy(source, target, load_sem.at[i])
        for i, (source, target) in enumerate((
            (patches_hbm, patches_ref), (vit_gain_hbm, vit_gain_ref), (fc1_hbm, fc1_ref), (fc2_hbm, fc2_ref),
            (merge_gain_hbm, merge_gain_ref), (mid_hbm, mid_w), (proj_hbm, proj_w), (owner_hbm, owner_ref), (live_hbm, live_ref)))
    ]
    for load in loads:
        load.start()

    def other(i):
        return lax.rem(here + 1 + lax.rem(i + ndp * 3 // 8, ndp - 1), ndp)

    def greet(i, carry):
        pl.semaphore_signal(barrier, inc=1, device_id={"dp": other(i)}, device_id_type=MESH)
        return carry

    lax.fori_loop(0, ndp - 1, greet, 0)

    def mlp(s):
        total = 4 * count
        to = lax.broadcasted_iota(jnp.int32, (total, total), 0)
        source = lax.broadcasted_iota(jnp.int32, (total, total), 1)
        order = (source == 4 * (to % count) + to // count).astype(BF16)
        ordered = dot(order, patches_ref[s * total : (s + 1) * total, :])
        rows[s] = ordered.astype(BF16).reshape(rows.shape[1:])
        normed = layer_norm(ordered, vit_gain_ref[...].reshape(1, width)).astype(BF16)
        up = dot_t(normed, fc1_ref[...])
        hidden = (up * jax.nn.sigmoid(1.702 * up)).astype(BF16)
        for h in range(HALVES):
            partial = dot(hidden, fc2_ref[:, h * part : (h + 1) * part]).reshape(own1.shape[2:])
            own1[s, h] = partial
            round1[s, h] = partial.astype(BF16)

    stages, halves = range(STAGES), range(HALVES)

    def turned(sides, chain):
        return sides if chain[1] % 2 == 0 else sides[::-1]

    chains = [(s, h) for s in stages for h in halves]
    sums1 = {
        c: Reduce(me, ring, turned(SUM1, c), own1.at[c], round1.at[c], relay1.at[c], got1.at[c], send1.at[c], recv1.at[c])
        for c in chains
    }
    gathers = {c: Gather(me, ring, turned(GATHER, c), chunks.at[c], send_g.at[c], recv_g.at[c], near_g.at[c]) for c in chains}
    sums2 = {
        c: Reduce(me, ring, turned(SUM2, c), own2.at[c], round2.at[c], relay2.at[c], got2.at[c], send2.at[c], recv2.at[c])
        for c in chains
    }

    for load in loads[:5]:
        load.wait()
    for s in stages:
        mlp(s)
        if s == 0:
            pl.semaphore_wait(barrier, 4 + ndp - 1)
        for h in halves:
            sums1[s, h].first()
    for k in range(1, sums1[0, 0].steps):
        for c in chains:
            sums1[c].step(k)
    for s in stages:
        summed = jnp.concatenate([sums1[s, h].last() for h in halves], axis=1)
        vit_out = (rows[s, me].astype(F32) + summed).astype(BF16)
        normed = layer_norm(vit_out.astype(F32), merge_gain_ref[...].reshape(1, width)).astype(BF16)
        for h in halves:
            chunks[s, h, me] = normed[:, h * part : (h + 1) * part]
            gathers[s, h].step(0)
    for k in range(1, gathers[0, 0].steps):
        for c in chains:
            gathers[c].step(k)
    for load in loads[5:]:
        load.wait()
    quarter = ring // 4
    for s in stages:
        turned_mid = jnp.zeros((mid_w.shape[0], count), F32)
        for h in halves:
            gathers[s, h].last()
            for j in range(4):
                block = chunks[s, h, quarter * j : quarter * (j + 1)].reshape(count, part)
                first = j * width + h * part
                turned_mid = turned_mid + dot_t(mid_w[:, first : first + part], block)
        middle = turned_mid.T
        middle = (0.5 * middle * (1.0 + lax.erf(middle * 0.7071067811865476))).astype(BF16)
        for t in range(ring):
            term = dot(middle, proj_w[:, t * emb : (t + 1) * emb])
            for h in halves:
                piece = term[h * (count // HALVES) : (h + 1) * (count // HALVES)]
                own2[s, h, t] = piece
                round2[s, h, t] = piece.astype(BF16)
        for h in halves:
            sums2[s, h].first()
    for k in range(1, sums2[0, 0].steps):
        for c in chains:
            sums2[c].step(k)

    owner = jnp.broadcast_to(owner_ref[...], (merged, merged))
    across = lax.broadcasted_iota(jnp.int32, (merged, merged), 1)
    down = lax.broadcasted_iota(jnp.int32, (merged, merged), 0)
    own_col = owner.astype(F32).T.astype(jnp.int32)
    slot = jnp.sum(jnp.where((owner == own_col) & (down < across), 1.0, 0.0), axis=0, keepdims=True)
    column = lax.broadcasted_iota(jnp.int32, (ndp, merged), 1)
    target = lax.broadcasted_iota(jnp.int32, (ndp, merged), 0)
    kept = (owner[:1] == target) & (column * 4 // (4 * merged // 4) < live_ref[0])
    placing = [jnp.where(kept & (slot == float(k)), 1.0, 0.0).astype(BF16) for k in (0, 1)]

    final = jnp.concatenate([sums2[c].last().astype(BF16) for c in chains], axis=0)
    lanes = outgoing.shape[2]
    for k in (0, 1):
        placed = dot(placing[k], final)
        for h in range(emb // lanes):
            outgoing[:, 2 * k + h, :] = placed[:, h * lanes : (h + 1) * lanes]

    def send(i, carry):
        peer = other(i)
        pltpu.make_async_remote_copy(
            src_ref=outgoing.at[peer], dst_ref=incoming.at[here], send_sem=send_x, recv_sem=recv_x,
            device_id={"dp": peer}, device_id_type=MESH).start()
        return carry

    lax.fori_loop(0, ndp - 1, send, 0)
    incoming[here] = outgoing[here]
    for c in chains:
        sums1[c].drain()
        gathers[c].drain()
        sums2[c].drain()
    others = pl.ds(0, ndp - 1)
    pltpu.make_async_copy(outgoing.at[others], incoming.at[others], send_x).wait()
    pltpu.make_async_copy(outgoing.at[others], incoming.at[others], recv_x).wait()

    row = lax.broadcasted_iota(jnp.int32, (2 * ndp, ndp), 0)
    origin = lax.broadcasted_iota(jnp.int32, (2 * ndp, ndp), 1)
    result = jnp.zeros((2 * ndp, emb), F32)
    for k in (0, 1):
        part = jnp.concatenate([incoming[:, 2 * k + h, :] for h in range(emb // lanes)], axis=1).astype(BF16)
        result = result + dot((row == 2 * origin + k).astype(BF16), part)
    out_ref[...] = result.astype(BF16)


def solution(mesh):
    ring, ndp = mesh.shape["tensor"], mesh.shape["dp"]

    def body(patches, live, owners, vit_gain, fc1, fc2, merge_gain, mid, proj):
        total, width = patches.shape
        chunk = total // STAGES // ring
        count = total // 4 // STAGES
        emb = proj.shape[1] // ring
        part, rows = width // HALVES, count // HALVES
        lead = (STAGES, HALVES)
        return pl.pallas_call(
            kernel,
            out_shape=jax.ShapeDtypeStruct((2 * ndp, emb), BF16),
            in_specs=[pl.BlockSpec(memory_space=pl.ANY)] * 9,
            out_specs=pl.BlockSpec(memory_space=pltpu.VMEM),
            scratch_shapes=[
                pltpu.SMEM((1,), jnp.int32),
                pltpu.VMEM((1, total // 4), jnp.int32),
                pltpu.VMEM((width,), F32),
                pltpu.VMEM((width,), F32),
                pltpu.VMEM(patches.shape, BF16),
                pltpu.VMEM(fc1.shape[::-1], BF16),
                pltpu.VMEM(fc2.shape, BF16),
                pltpu.VMEM(mid.shape[::-1], BF16),
                pltpu.VMEM(proj.shape, BF16),
                pltpu.VMEM((STAGES, ring, chunk, width), BF16),
                pltpu.VMEM(lead + (ring, chunk, part), F32),
                pltpu.VMEM(lead + (ring, chunk, part), BF16),
                pltpu.VMEM(lead + (2, DEPTH, chunk, part), BF16),
                pltpu.VMEM(lead + (2, DEPTH, 2, chunk, part), BF16),
                pltpu.VMEM(lead + (ring, chunk, part), BF16),
                pltpu.VMEM(lead + (ring, rows, emb), F32),
                pltpu.VMEM(lead + (ring, rows, emb), BF16),
                pltpu.VMEM(lead + (2, DEPTH, rows, emb), BF16),
                pltpu.VMEM(lead + (2, DEPTH, 2, rows, emb), BF16),
                pltpu.VMEM((ndp, 2 * emb // 128, 128), F32),
                pltpu.VMEM((ndp, 2 * emb // 128, 128), F32),
                pltpu.SemaphoreType.DMA((9,)),
            ]
            + [pltpu.SemaphoreType.DMA(lead), pltpu.SemaphoreType.DMA(lead + (2, DEPTH))] * 2
            + [pltpu.SemaphoreType.DMA(lead)] * 2
            + [pltpu.SemaphoreType.DMA(lead + (2, DEPTH))]
            + [pltpu.SemaphoreType.DMA, pltpu.SemaphoreType.DMA],
            compiler_params=pltpu.CompilerParams(
                collective_id=0, has_side_effects=True, vmem_limit_bytes=56 * 2**20
            ),
            name="vision_block",
        )(live, owners.reshape(1, total // 4), vit_gain, merge_gain, patches, fc1.T, fc2, mid.T, proj)

    return jax.shard_map(
        body,
        mesh=mesh,
        in_specs=(
            P("dp", None), P("dp"), P("dp", None), P(), P(None, "tensor"), P("tensor", None), P(),
            P(None, "tensor"), P("tensor", None),
        ),
        out_specs=P("dp", "tensor"),
        check_vma=False,
    )
```

```python
import functools

import jax
import jax.numpy as jnp
from jax import lax
from jax.experimental import pallas as pl
from jax.experimental.pallas import tpu as pltpu
from jax.sharding import PartitionSpec as P

MESH = pl.DeviceIdType.MESH
F32 = jnp.float32
BF16 = jnp.bfloat16
STAGES = 2
HALVES = 2
SIGNS = (1, -1)
SUM1 = ((2, 2, 2, 2), (1, 2, 2, 2))
GATHER = ((2, 2, 2, 2), (2, 2, 2, 1))
SUM2 = ((2, 2, 2, 2), (1, 2, 2, 2))
DEPTH = 4
LAG = 0


def dot(a, b):
    return jnp.dot(a, b, preferred_element_type=F32)


def dot_t(a, b):
    return lax.dot_general(a, b, (((1,), (1,)), ((), ())), preferred_element_type=F32)


def layer_norm(values, gain):
    mean = jnp.mean(values, axis=-1, keepdims=True)
    centered = values - mean
    variance = jnp.mean(centered * centered, axis=-1, keepdims=True)
    return centered * lax.rsqrt(variance + 1e-06) * gain


def positions(hops):
    left, places = sum(hops), []
    for hop in hops:
        places.append(left)
        left -= hop
    return places


class Reduce:
    def __init__(self, me, ring, sides, own, rounded, relay, got, send_sem, recv_sem):
        self.me, self.ring, self.sides = me, ring, sides
        self.places = [positions(hops) for hops in sides]
        self.own, self.rounded, self.relay = own, rounded, relay
        self.got = got
        self.send_sem, self.recv_sem = send_sem, recv_sem
        self.steps = max(len(hops) for hops in sides)

    def place(self, steps):
        return lax.rem(self.me + (steps + self.ring), self.ring)

    def far(self, d, k):
        source = self.relay.at[d, k] if k else self.rounded.at[self.place(self.places[d][0] * SIGNS[d])]
        return pltpu.make_async_remote_copy(
            src_ref=source, dst_ref=self.got.at[d, k, 0],
            send_sem=self.send_sem, recv_sem=self.recv_sem.at[d, k],
            device_id={"tensor": self.place(self.sides[d][k] * SIGNS[d])}, device_id_type=MESH)

    def has_near(self, d, k):
        return k < len(self.sides[d]) and self.sides[d][k] == 2

    def near(self, d, k):
        return pltpu.make_async_remote_copy(
            src_ref=self.rounded.at[self.place((self.places[d][k] - 1) * SIGNS[d])], dst_ref=self.got.at[d, k, 1],
            send_sem=self.send_sem, recv_sem=self.recv_sem.at[d, k],
            device_id={"tensor": self.place(SIGNS[d])}, device_id_type=MESH)

    def first(self):
        for d in (0, 1):
            self.far(d, 0).start()
        for k in (0, 1):
            for d in (0, 1):
                if self.has_near(d, k):
                    self.near(d, k).start()

    def arrived(self, d, k):
        if not self.has_near(d, k):
            self.far(d, k).wait_recv()
            return self.got[d, k, 0].astype(F32)
        both = self.got.at[d, k]
        pltpu.make_async_copy(both, both, self.recv_sem.at[d, k]).wait()
        return self.got[d, k, 0].astype(F32) + self.got[d, k, 1].astype(F32)

    def step(self, k):
        for d in (0, 1):
            if k < len(self.sides[d]):
                got = self.arrived(d, k - 1)
                mine = self.own[self.place(self.places[d][k] * SIGNS[d])]
                self.relay[d, k] = (mine + got).astype(BF16)
                self.far(d, k).start()
                if self.has_near(d, k + 1):
                    self.near(d, k + 1).start()

    def last(self):
        return self.own[self.me] + self.arrived(0, len(self.sides[0]) - 1) + self.arrived(1, len(self.sides[1]) - 1)

    def drain(self):
        every = self.rounded.at[pl.ds(0, self.ring - 1)]
        pltpu.make_async_copy(every, every, self.send_sem).wait()


class Gather:
    def __init__(self, me, ring, sides, chunks, send_sem, recv_sem, near_sem):
        self.me, self.ring, self.sides, self.chunks = me, ring, sides, chunks
        self.send_sem, self.recv_sem, self.near_sem = send_sem, recv_sem, near_sem
        self.steps = max(len(hops) for hops in sides)

    def place(self, steps):
        return lax.rem(self.me + (steps + self.ring), self.ring)

    def copy(self, d, k, hop, distance):
        chunk = self.chunks.at[self.place(-distance * SIGNS[d])]
        return pltpu.make_async_remote_copy(
            src_ref=chunk, dst_ref=chunk, send_sem=self.send_sem,
            recv_sem=self.near_sem if hop < self.sides[d][k] else self.recv_sem.at[d, k],
            device_id={"tensor": self.place(hop * SIGNS[d])}, device_id_type=MESH)

    def sent(self, d, k, hop):
        return self.copy(d, k, hop, sum(self.sides[d][:k]))

    def landed(self, d, k, hop):
        return self.copy(d, k, hop, sum(self.sides[d][:k]) + hop)

    def step(self, k):
        live = [d for d in (0, 1) if k < len(self.sides[d])]
        for d in live:
            if k > 0:
                self.landed(d, k - 1, self.sides[d][k - 1]).wait_recv()
            self.sent(d, k, self.sides[d][k]).start()
        for d in live:
            if self.sides[d][k] == 2:
                self.sent(d, k, 1).start()

    def last(self):
        for d in (0, 1):
            k = len(self.sides[d]) - 1
            self.landed(d, k, self.sides[d][k]).wait_recv()
        between = self.chunks.at[pl.ds(0, sum(hops.count(2) for hops in self.sides))]
        pltpu.make_async_copy(between, between, self.near_sem).wait()

    def drain(self):
        every = self.chunks.at[pl.ds(0, self.ring - 1)]
        pltpu.make_async_copy(every, every, self.send_sem).wait()


def kernel(
    live_hbm, owner_hbm, vit_gain_hbm, merge_gain_hbm, patches_hbm, fc1_hbm, fc2_hbm, mid_hbm, proj_hbm,
    out_ref,
    live_ref, owner_ref, vit_gain_ref, merge_gain_ref, patches_ref, fc1_ref, fc2_ref, mid_w, proj_w,
    rows, own1, round1, relay1, got1, chunks, own2, round2, relay2, got2,
    outgoing, incoming,
    load_sem, send1, recv1, send_g, recv_g, near_g, send2, recv2, send_x, recv_x,
):
    ring = lax.axis_size("tensor")
    ndp = lax.axis_size("dp")
    me = lax.axis_index("tensor")
    here = lax.axis_index("dp")
    merged = patches_ref.shape[0] // 4
    count = merged // STAGES
    width = patches_ref.shape[1]
    part = width // HALVES
    emb = own2.shape[4]

    barrier = pltpu.get_barrier_semaphore()
    for hops in (1, 2, ring - 2, ring - 1):
        pl.semaphore_signal(barrier, inc=1, device_id={"tensor": lax.rem(me + hops, ring)}, device_id_type=MESH)
    half = patches_ref.shape[0] // STAGES
    loads = [
        pltpu.make_async_copy(source, target, load_sem.at[i])
        for i, (source, target) in enumerate((
            (patches_hbm.at[pl.ds(0, half)], patches_ref.at[pl.ds(0, half)]), (vit_gain_hbm, vit_gain_ref),
            (fc1_hbm, fc1_ref), (fc2_hbm, fc2_ref),
            (patches_hbm.at[pl.ds(half, half)], patches_ref.at[pl.ds(half, half)]), (merge_gain_hbm, merge_gain_ref),
            (mid_hbm, mid_w), (proj_hbm, proj_w), (owner_hbm, owner_ref), (live_hbm, live_ref)))
    ]
    for load in loads[:4]:
        load.start()

    def other(i):
        return lax.rem(here + 1 + lax.rem(i + ndp * 3 // 8, ndp - 1), ndp)

    def greet(i, carry):
        pl.semaphore_signal(barrier, inc=1, device_id={"dp": other(i)}, device_id_type=MESH)
        return carry

    lax.fori_loop(0, ndp - 1, greet, 0)

    def mlp(s):
        total = 4 * count
        to = lax.broadcasted_iota(jnp.int32, (total, total), 0)
        source = lax.broadcasted_iota(jnp.int32, (total, total), 1)
        order = (source == 4 * (to % count) + to // count).astype(BF16)
        ordered = dot(order, patches_ref[s * total : (s + 1) * total, :])
        rows[s] = ordered.astype(BF16).reshape(rows.shape[1:])
        normed = layer_norm(ordered, vit_gain_ref[...].reshape(1, width)).astype(BF16)
        up = dot_t(normed, fc1_ref[...])
        hidden = (up * jax.nn.sigmoid(1.702 * up)).astype(BF16)
        for h in range(HALVES):
            partial = dot(hidden, fc2_ref[:, h * part : (h + 1) * part]).reshape(own1.shape[2:])
            own1[s, h] = partial
            round1[s, h] = partial.astype(BF16)

    stages, halves = range(STAGES), range(HALVES)

    def turned(sides, chain):
        return sides if chain[1] % 2 == 0 else sides[::-1]

    chains = [(s, h) for s in stages for h in halves]
    sums1 = {
        c: Reduce(me, ring, turned(SUM1, c), own1.at[c], round1.at[c], relay1.at[c], got1.at[c], send1.at[c], recv1.at[c])
        for c in chains
    }
    gathers = {c: Gather(me, ring, turned(GATHER, c), chunks.at[c], send_g.at[c], recv_g.at[c], near_g.at[c]) for c in chains}
    sums2 = {
        c: Reduce(me, ring, turned(SUM2, c), own2.at[c], round2.at[c], relay2.at[c], got2.at[c], send2.at[c], recv2.at[c])
        for c in chains
    }

    for load in loads[:4]:
        load.wait()
    for load in loads[4:]:
        load.start()

    def start_sum1(s):
        if s == 1:
            for load in loads[4:6]:
                load.wait()
        mlp(s)
        if s == 0:
            pl.semaphore_wait(barrier, 4 + ndp - 1)
        for h in halves:
            sums1[s, h].first()

    def start_gather(s):
        summed = jnp.concatenate([sums1[s, h].last() for h in halves], axis=1)
        vit_out = (rows[s, me].astype(F32) + summed).astype(BF16)
        normed = layer_norm(vit_out.astype(F32), merge_gain_ref[...].reshape(1, width)).astype(BF16)
        for h in halves:
            chunks[s, h, me] = normed[:, h * part : (h + 1) * part]
            gathers[s, h].step(0)

    def start_sum2(s):
        if s == 0:
            for load in loads[6:]:
                load.wait()
        quarter = ring // 4
        turned_mid = jnp.zeros((mid_w.shape[0], count), F32)
        for h in halves:
            gathers[s, h].last()
            for j in range(4):
                block = chunks[s, h, quarter * j : quarter * (j + 1)].reshape(count, part)
                first = j * width + h * part
                turned_mid = turned_mid + dot_t(mid_w[:, first : first + part], block)
        middle = turned_mid.T
        middle = (0.5 * middle * (1.0 + lax.erf(middle * 0.7071067811865476))).astype(BF16)
        for t in range(ring):
            term = dot(middle, proj_w[:, t * emb : (t + 1) * emb])
            for h in halves:
                piece = term[h * (count // HALVES) : (h + 1) * (count // HALVES)]
                own2[s, h, t] = piece
                round2[s, h, t] = piece.astype(BF16)
        for h in halves:
            sums2[s, h].first()

    def steps_of(group, s):
        def advance(k):
            for h in halves:
                group[s, h].step(k)

        return [functools.partial(advance, k) for k in range(1, group[s, 0].steps)]

    events = [
        [functools.partial(start_sum1, s)] + steps_of(sums1, s)
        + [functools.partial(start_gather, s)] + steps_of(gathers, s)
        + [functools.partial(start_sum2, s)] + steps_of(sums2, s)
        for s in stages
    ]
    for turn in range(len(events[0]) + LAG * (STAGES - 1)):
        for s in stages:
            if 0 <= turn - LAG * s < len(events[s]):
                events[s][turn - LAG * s]()

    owner = jnp.broadcast_to(owner_ref[...], (merged, merged))
    across = lax.broadcasted_iota(jnp.int32, (merged, merged), 1)
    down = lax.broadcasted_iota(jnp.int32, (merged, merged), 0)
    own_col = owner.astype(F32).T.astype(jnp.int32)
    slot = jnp.sum(jnp.where((owner == own_col) & (down < across), 1.0, 0.0), axis=0, keepdims=True)
    column = lax.broadcasted_iota(jnp.int32, (ndp, merged), 1)
    target = lax.broadcasted_iota(jnp.int32, (ndp, merged), 0)
    kept = (owner[:1] == target) & (column * 4 // (4 * merged // 4) < live_ref[0])
    placing = [jnp.where(kept & (slot == float(k)), 1.0, 0.0).astype(BF16) for k in (0, 1)]

    final = jnp.concatenate([sums2[c].last().astype(BF16) for c in chains], axis=0)
    lanes = outgoing.shape[2]
    for k in (0, 1):
        placed = dot(placing[k], final)
        for h in range(emb // lanes):
            outgoing[:, 2 * k + h, :] = placed[:, h * lanes : (h + 1) * lanes].astype(BF16)

    def send(i, carry):
        peer = other(i)
        pltpu.make_async_remote_copy(
            src_ref=outgoing.at[peer], dst_ref=incoming.at[here], send_sem=send_x, recv_sem=recv_x,
            device_id={"dp": peer}, device_id_type=MESH).start()
        return carry

    lax.fori_loop(0, ndp - 1, send, 0)
    incoming[here] = outgoing[here]
    for c in chains:
        sums1[c].drain()
        gathers[c].drain()
        sums2[c].drain()
    others = pl.ds(0, ndp - 1)
    pltpu.make_async_copy(outgoing.at[others], incoming.at[others], send_x).wait()
    pltpu.make_async_copy(outgoing.at[others], incoming.at[others], recv_x).wait()

    row = lax.broadcasted_iota(jnp.int32, (2 * ndp, ndp), 0)
    origin = lax.broadcasted_iota(jnp.int32, (2 * ndp, ndp), 1)
    result = jnp.zeros((2 * ndp, emb), F32)
    for k in (0, 1):
        part = jnp.concatenate([incoming[:, 2 * k + h, :] for h in range(emb // lanes)], axis=1)
        result = result + dot((row == 2 * origin + k).astype(BF16), part)
    out_ref[...] = result.astype(BF16)


def solution(mesh):
    ring, ndp = mesh.shape["tensor"], mesh.shape["dp"]

    def body(patches, live, owners, vit_gain, fc1, fc2, merge_gain, mid, proj):
        total, width = patches.shape
        chunk = total // STAGES // ring
        count = total // 4 // STAGES
        emb = proj.shape[1] // ring
        part, rows = width // HALVES, count // HALVES
        lead = (STAGES, HALVES)
        return pl.pallas_call(
            kernel,
            out_shape=jax.ShapeDtypeStruct((2 * ndp, emb), BF16),
            in_specs=[pl.BlockSpec(memory_space=pl.ANY)] * 9,
            out_specs=pl.BlockSpec(memory_space=pltpu.VMEM),
            scratch_shapes=[
                pltpu.SMEM((1,), jnp.int32),
                pltpu.VMEM((1, total // 4), jnp.int32),
                pltpu.VMEM((width,), F32),
                pltpu.VMEM((width,), F32),
                pltpu.VMEM(patches.shape, BF16),
                pltpu.VMEM(fc1.shape[::-1], BF16),
                pltpu.VMEM(fc2.shape, BF16),
                pltpu.VMEM(mid.shape[::-1], BF16),
                pltpu.VMEM(proj.shape, BF16),
                pltpu.VMEM((STAGES, ring, chunk, width), BF16),
                pltpu.VMEM(lead + (ring, chunk, part), F32),
                pltpu.VMEM(lead + (ring, chunk, part), BF16),
                pltpu.VMEM(lead + (2, DEPTH, chunk, part), BF16),
                pltpu.VMEM(lead + (2, DEPTH, 2, chunk, part), BF16),
                pltpu.VMEM(lead + (ring, chunk, part), BF16),
                pltpu.VMEM(lead + (ring, rows, emb), F32),
                pltpu.VMEM(lead + (ring, rows, emb), BF16),
                pltpu.VMEM(lead + (2, DEPTH, rows, emb), BF16),
                pltpu.VMEM(lead + (2, DEPTH, 2, rows, emb), BF16),
                pltpu.VMEM((ndp, 2 * emb // 128, 128), BF16),
                pltpu.VMEM((ndp, 2 * emb // 128, 128), BF16),
                pltpu.SemaphoreType.DMA((10,)),
            ]
            + [pltpu.SemaphoreType.DMA(lead), pltpu.SemaphoreType.DMA(lead + (2, DEPTH))] * 2
            + [pltpu.SemaphoreType.DMA(lead)] * 2
            + [pltpu.SemaphoreType.DMA(lead + (2, DEPTH))]
            + [pltpu.SemaphoreType.DMA, pltpu.SemaphoreType.DMA],
            compiler_params=pltpu.CompilerParams(
                collective_id=0, has_side_effects=True, vmem_limit_bytes=56 * 2**20
            ),
            name="vision_block",
        )(live, owners.reshape(1, total // 4), vit_gain, merge_gain, patches, fc1.T, fc2, mid.T, proj)

    return jax.shard_map(
        body,
        mesh=mesh,
        in_specs=(
            P("dp", None), P("dp"), P("dp", None), P(), P(None, "tensor"), P("tensor", None), P(),
            P(None, "tensor"), P("tensor", None),
        ),
        out_specs=P("dp", "tensor"),
        check_vma=False,
    )
```

```python
import functools

import jax
import jax.numpy as jnp
from jax import lax
from jax.experimental import pallas as pl
from jax.experimental.pallas import tpu as pltpu
from jax.sharding import PartitionSpec as P

MESH = pl.DeviceIdType.MESH
F32 = jnp.float32
BF16 = jnp.bfloat16
STAGES = 2
HALVES = 2
SIGNS = (1, -1)
SUM1 = ((2, 2, 2, 2), (1, 2, 2, 2))
GATHER = ((2, 2, 2, 2), (2, 2, 2, 1))
SUM2 = ((2, 2, 2, 2), (1, 2, 2, 2))
DEPTH = 4
LAG = 0


def dot(a, b):
    return jnp.dot(a, b, preferred_element_type=F32)


def dot_t(a, b):
    return lax.dot_general(a, b, (((1,), (1,)), ((), ())), preferred_element_type=F32)


def layer_norm(values, gain):
    mean = jnp.mean(values, axis=-1, keepdims=True)
    centered = values - mean
    variance = jnp.mean(centered * centered, axis=-1, keepdims=True)
    return centered * lax.rsqrt(variance + 1e-06) * gain


def positions(hops):
    left, places = sum(hops), []
    for hop in hops:
        places.append(left)
        left -= hop
    return places


class Reduce:
    def __init__(self, me, ring, sides, own, rounded, relay, got, send_sem, recv_sem):
        self.me, self.ring, self.sides = me, ring, sides
        self.places = [positions(hops) for hops in sides]
        self.own, self.rounded, self.relay = own, rounded, relay
        self.got = got
        self.send_sem, self.recv_sem = send_sem, recv_sem
        self.steps = max(len(hops) for hops in sides)

    def place(self, steps):
        return lax.rem(self.me + (steps + self.ring), self.ring)

    def far(self, d, k):
        source = self.relay.at[d, k] if k else self.rounded.at[self.place(self.places[d][0] * SIGNS[d])]
        return pltpu.make_async_remote_copy(
            src_ref=source, dst_ref=self.got.at[d, k, 0],
            send_sem=self.send_sem, recv_sem=self.recv_sem.at[d, k],
            device_id={"tensor": self.place(self.sides[d][k] * SIGNS[d])}, device_id_type=MESH)

    def has_near(self, d, k):
        return k < len(self.sides[d]) and self.sides[d][k] == 2

    def near(self, d, k):
        return pltpu.make_async_remote_copy(
            src_ref=self.rounded.at[self.place((self.places[d][k] - 1) * SIGNS[d])], dst_ref=self.got.at[d, k, 1],
            send_sem=self.send_sem, recv_sem=self.recv_sem.at[d, k],
            device_id={"tensor": self.place(SIGNS[d])}, device_id_type=MESH)

    def first(self):
        for d in (0, 1):
            self.far(d, 0).start()
        for k in (0, 1):
            for d in (0, 1):
                if self.has_near(d, k):
                    self.near(d, k).start()

    def arrived(self, d, k):
        if not self.has_near(d, k):
            self.far(d, k).wait_recv()
            return self.got[d, k, 0].astype(F32)
        both = self.got.at[d, k]
        pltpu.make_async_copy(both, both, self.recv_sem.at[d, k]).wait()
        return self.got[d, k, 0].astype(F32) + self.got[d, k, 1].astype(F32)

    def step(self, k):
        for d in (0, 1):
            if k < len(self.sides[d]):
                got = self.arrived(d, k - 1)
                mine = self.own[self.place(self.places[d][k] * SIGNS[d])]
                self.relay[d, k] = (mine + got).astype(BF16)
                self.far(d, k).start()
                if self.has_near(d, k + 1):
                    self.near(d, k + 1).start()

    def last(self):
        return self.own[self.me] + self.arrived(0, len(self.sides[0]) - 1) + self.arrived(1, len(self.sides[1]) - 1)

    def drain(self):
        every = self.rounded.at[pl.ds(0, self.ring - 1)]
        pltpu.make_async_copy(every, every, self.send_sem).wait()


class Gather:
    def __init__(self, me, ring, sides, chunks, send_sem, recv_sem, near_sem):
        self.me, self.ring, self.sides, self.chunks = me, ring, sides, chunks
        self.send_sem, self.recv_sem, self.near_sem = send_sem, recv_sem, near_sem
        self.steps = max(len(hops) for hops in sides)

    def place(self, steps):
        return lax.rem(self.me + (steps + self.ring), self.ring)

    def copy(self, d, k, hop, distance):
        chunk = self.chunks.at[self.place(-distance * SIGNS[d])]
        return pltpu.make_async_remote_copy(
            src_ref=chunk, dst_ref=chunk, send_sem=self.send_sem,
            recv_sem=self.near_sem if hop < self.sides[d][k] else self.recv_sem.at[d, k],
            device_id={"tensor": self.place(hop * SIGNS[d])}, device_id_type=MESH)

    def sent(self, d, k, hop):
        return self.copy(d, k, hop, sum(self.sides[d][:k]))

    def landed(self, d, k, hop):
        return self.copy(d, k, hop, sum(self.sides[d][:k]) + hop)

    def step(self, k):
        live = [d for d in (0, 1) if k < len(self.sides[d])]
        for d in live:
            if k > 0:
                self.landed(d, k - 1, self.sides[d][k - 1]).wait_recv()
            self.sent(d, k, self.sides[d][k]).start()
        for d in live:
            if self.sides[d][k] == 2:
                self.sent(d, k, 1).start()

    def last(self):
        for d in (0, 1):
            k = len(self.sides[d]) - 1
            self.landed(d, k, self.sides[d][k]).wait_recv()
        between = self.chunks.at[pl.ds(0, sum(hops.count(2) for hops in self.sides))]
        pltpu.make_async_copy(between, between, self.near_sem).wait()

    def drain(self):
        every = self.chunks.at[pl.ds(0, self.ring - 1)]
        pltpu.make_async_copy(every, every, self.send_sem).wait()


def kernel(
    live_hbm, owner_hbm, vit_gain_hbm, merge_gain_hbm, patches_hbm, fc1_hbm, fc2_hbm, mid_hbm, proj_hbm,
    out_ref,
    live_ref, owner_ref, vit_gain_ref, merge_gain_ref, patches_ref, fc1_ref, fc2_ref, mid_w, proj_w,
    rows, own1, round1, relay1, got1, chunks, own2, round2, relay2, got2,
    outgoing, incoming,
    load_sem, send1, recv1, send_g, recv_g, near_g, send2, recv2, send_x, recv_x,
):
    ring = lax.axis_size("tensor")
    ndp = lax.axis_size("dp")
    me = lax.axis_index("tensor")
    here = lax.axis_index("dp")
    merged = patches_ref.shape[0] // 4
    count = merged // STAGES
    width = patches_ref.shape[1]
    part = width // HALVES
    emb = own2.shape[4]

    barrier = pltpu.get_barrier_semaphore()
    for hops in (1, 2, ring - 2, ring - 1):
        pl.semaphore_signal(barrier, inc=1, device_id={"tensor": lax.rem(me + hops, ring)}, device_id_type=MESH)
    half = patches_ref.shape[0] // STAGES
    loads = [
        pltpu.make_async_copy(source, target, load_sem.at[i])
        for i, (source, target) in enumerate((
            (patches_hbm.at[pl.ds(0, half)], patches_ref.at[pl.ds(0, half)]), (vit_gain_hbm, vit_gain_ref),
            (fc1_hbm, fc1_ref), (fc2_hbm, fc2_ref),
            (patches_hbm.at[pl.ds(half, half)], patches_ref.at[pl.ds(half, half)]), (merge_gain_hbm, merge_gain_ref),
            (mid_hbm, mid_w), (proj_hbm, proj_w), (owner_hbm, owner_ref), (live_hbm, live_ref)))
    ]
    for load in loads[:4]:
        load.start()

    def other(i):
        return lax.rem(here + 1 + lax.rem(i + ndp * 3 // 8, ndp - 1), ndp)

    def greet(i, carry):
        pl.semaphore_signal(barrier, inc=1, device_id={"dp": other(i)}, device_id_type=MESH)
        return carry

    lax.fori_loop(0, ndp - 1, greet, 0)

    def mlp(s):
        total = 4 * count
        to = lax.broadcasted_iota(jnp.int32, (total, total), 0)
        source = lax.broadcasted_iota(jnp.int32, (total, total), 1)
        order = (source == 4 * (to % count) + to // count).astype(BF16)
        ordered = dot(order, patches_ref[s * total : (s + 1) * total, :])
        rows[s] = ordered.astype(BF16).reshape(rows.shape[1:])
        normed = layer_norm(ordered, vit_gain_ref[...].reshape(1, width)).astype(BF16)
        up = dot_t(normed, fc1_ref[...])
        hidden = (up * jax.nn.sigmoid(1.702 * up)).astype(BF16)
        for h in range(HALVES):
            partial = dot(hidden, fc2_ref[:, h * part : (h + 1) * part]).reshape(own1.shape[2:])
            own1[s, h] = partial
            round1[s, h] = partial.astype(BF16)

    stages, halves = range(STAGES), range(HALVES)

    def turned(sides, chain):
        return sides if chain[1] % 2 == 0 else sides[::-1]

    chains = [(s, h) for s in stages for h in halves]
    sums1 = {
        c: Reduce(me, ring, turned(SUM1, c), own1.at[c], round1.at[c], relay1.at[c], got1.at[c], send1.at[c], recv1.at[c])
        for c in chains
    }
    gathers = {c: Gather(me, ring, turned(GATHER, c), chunks.at[c], send_g.at[c], recv_g.at[c], near_g.at[c]) for c in chains}
    sums2 = {
        c: Reduce(me, ring, turned(SUM2, c), own2.at[c], round2.at[c], relay2.at[c], got2.at[c], send2.at[c], recv2.at[c])
        for c in chains
    }

    for load in loads[:4]:
        load.wait()
    for load in loads[4:]:
        load.start()

    def start_sum1(s):
        if s == 1:
            for load in loads[4:6]:
                load.wait()
        mlp(s)
        if s == 0:
            pl.semaphore_wait(barrier, 4 + ndp - 1)
        for h in halves:
            sums1[s, h].first()

    def start_gather(s):
        summed = jnp.concatenate([sums1[s, h].last() for h in halves], axis=1)
        vit_out = (rows[s, me].astype(F32) + summed).astype(BF16)
        normed = layer_norm(vit_out.astype(F32), merge_gain_ref[...].reshape(1, width)).astype(BF16)
        for h in halves:
            chunks[s, h, me] = normed[:, h * part : (h + 1) * part]
            gathers[s, h].step(0)

    def start_sum2(s):
        if s == 0:
            for load in loads[6:]:
                load.wait()
        quarter = ring // 4
        turned_mid = jnp.zeros((mid_w.shape[0], count), F32)
        for h in halves:
            gathers[s, h].last()
            for j in range(4):
                block = chunks[s, h, quarter * j : quarter * (j + 1)].reshape(count, part)
                first = j * width + h * part
                turned_mid = turned_mid + dot_t(mid_w[:, first : first + part], block)
        middle = turned_mid.T
        middle = (0.5 * middle * (1.0 + lax.erf(middle * 0.7071067811865476))).astype(BF16)
        for t in range(ring):
            term = dot(middle, proj_w[:, t * emb : (t + 1) * emb])
            for h in halves:
                piece = term[h * (count // HALVES) : (h + 1) * (count // HALVES)]
                own2[s, h, t] = piece
                round2[s, h, t] = piece.astype(BF16)
        for h in halves:
            sums2[s, h].first()

    def steps_of(group, s):
        def advance(k):
            for h in halves:
                group[s, h].step(k)

        return [functools.partial(advance, k) for k in range(1, group[s, 0].steps)]

    events = [
        [functools.partial(start_sum1, s)] + steps_of(sums1, s)
        + [functools.partial(start_gather, s)] + steps_of(gathers, s)
        + [functools.partial(start_sum2, s)] + steps_of(sums2, s)
        for s in stages
    ]
    for turn in range(len(events[0]) + LAG * (STAGES - 1)):
        for s in stages:
            if 0 <= turn - LAG * s < len(events[s]):
                events[s][turn - LAG * s]()

    owner = jnp.broadcast_to(owner_ref[...], (merged, merged))
    across = lax.broadcasted_iota(jnp.int32, (merged, merged), 1)
    down = lax.broadcasted_iota(jnp.int32, (merged, merged), 0)
    own_col = owner.astype(F32).T.astype(jnp.int32)
    slot = jnp.sum(jnp.where((owner == own_col) & (down < across), 1.0, 0.0), axis=0, keepdims=True)
    column = lax.broadcasted_iota(jnp.int32, (ndp, merged), 1)
    target = lax.broadcasted_iota(jnp.int32, (ndp, merged), 0)
    kept = (owner[:1] == target) & (column * 4 // (4 * merged // 4) < live_ref[0])
    placing = [jnp.where(kept & (slot == float(k)), 1.0, 0.0).astype(BF16) for k in (0, 1)]

    final = jnp.concatenate([sums2[c].last().astype(BF16) for c in chains], axis=0)
    lanes = outgoing.shape[2]
    for k in (0, 1):
        placed = dot(placing[k], final)
        for h in range(emb // lanes):
            outgoing[:, 2 * k + h, :] = placed[:, h * lanes : (h + 1) * lanes]

    def send(i, carry):
        peer = other(i)
        pltpu.make_async_remote_copy(
            src_ref=outgoing.at[peer], dst_ref=incoming.at[here], send_sem=send_x, recv_sem=recv_x,
            device_id={"dp": peer}, device_id_type=MESH).start()
        return carry

    lax.fori_loop(0, ndp - 1, send, 0)
    incoming[here] = outgoing[here]
    for c in chains:
        sums1[c].drain()
        gathers[c].drain()
        sums2[c].drain()
    others = pl.ds(0, ndp - 1)
    pltpu.make_async_copy(outgoing.at[others], incoming.at[others], send_x).wait()
    pltpu.make_async_copy(outgoing.at[others], incoming.at[others], recv_x).wait()

    row = lax.broadcasted_iota(jnp.int32, (2 * ndp, ndp), 0)
    origin = lax.broadcasted_iota(jnp.int32, (2 * ndp, ndp), 1)
    result = jnp.zeros((2 * ndp, emb), F32)
    for k in (0, 1):
        part = jnp.concatenate([incoming[:, 2 * k + h, :] for h in range(emb // lanes)], axis=1).astype(BF16)
        result = result + dot((row == 2 * origin + k).astype(BF16), part)
    out_ref[...] = result.astype(BF16)


def solution(mesh):
    ring, ndp = mesh.shape["tensor"], mesh.shape["dp"]

    def body(patches, live, owners, vit_gain, fc1, fc2, merge_gain, mid, proj):
        total, width = patches.shape
        chunk = total // STAGES // ring
        count = total // 4 // STAGES
        emb = proj.shape[1] // ring
        part, rows = width // HALVES, count // HALVES
        lead = (STAGES, HALVES)
        return pl.pallas_call(
            kernel,
            out_shape=jax.ShapeDtypeStruct((2 * ndp, emb), BF16),
            in_specs=[pl.BlockSpec(memory_space=pl.ANY)] * 9,
            out_specs=pl.BlockSpec(memory_space=pltpu.VMEM),
            scratch_shapes=[
                pltpu.SMEM((1,), jnp.int32),
                pltpu.VMEM((1, total // 4), jnp.int32),
                pltpu.VMEM((width,), F32),
                pltpu.VMEM((width,), F32),
                pltpu.VMEM(patches.shape, BF16),
                pltpu.VMEM(fc1.shape[::-1], BF16),
                pltpu.VMEM(fc2.shape, BF16),
                pltpu.VMEM(mid.shape[::-1], BF16),
                pltpu.VMEM(proj.shape, BF16),
                pltpu.VMEM((STAGES, ring, chunk, width), BF16),
                pltpu.VMEM(lead + (ring, chunk, part), F32),
                pltpu.VMEM(lead + (ring, chunk, part), BF16),
                pltpu.VMEM(lead + (2, DEPTH, chunk, part), BF16),
                pltpu.VMEM(lead + (2, DEPTH, 2, chunk, part), BF16),
                pltpu.VMEM(lead + (ring, chunk, part), BF16),
                pltpu.VMEM(lead + (ring, rows, emb), F32),
                pltpu.VMEM(lead + (ring, rows, emb), BF16),
                pltpu.VMEM(lead + (2, DEPTH, rows, emb), BF16),
                pltpu.VMEM(lead + (2, DEPTH, 2, rows, emb), BF16),
                pltpu.VMEM((ndp, 2 * emb // 128, 128), F32),
                pltpu.VMEM((ndp, 2 * emb // 128, 128), F32),
                pltpu.SemaphoreType.DMA((10,)),
            ]
            + [pltpu.SemaphoreType.DMA(lead), pltpu.SemaphoreType.DMA(lead + (2, DEPTH))] * 2
            + [pltpu.SemaphoreType.DMA(lead)] * 2
            + [pltpu.SemaphoreType.DMA(lead + (2, DEPTH))]
            + [pltpu.SemaphoreType.DMA, pltpu.SemaphoreType.DMA],
            compiler_params=pltpu.CompilerParams(
                collective_id=0, has_side_effects=True, vmem_limit_bytes=56 * 2**20
            ),
            name="vision_block",
        )(live, owners.reshape(1, total // 4), vit_gain, merge_gain, patches, fc1.T, fc2, mid.T, proj)

    return jax.shard_map(
        body,
        mesh=mesh,
        in_specs=(
            P("dp", None), P("dp"), P("dp", None), P(), P(None, "tensor"), P("tensor", None), P(),
            P(None, "tensor"), P("tensor", None),
        ),
        out_specs=P("dp", "tensor"),
        check_vma=False,
    )
```

```python
import functools

import jax
import jax.numpy as jnp
from jax import lax
from jax.experimental import pallas as pl
from jax.experimental.pallas import tpu as pltpu
from jax.sharding import PartitionSpec as P

MESH = pl.DeviceIdType.MESH
F32 = jnp.float32
BF16 = jnp.bfloat16
STAGES = 2
HALVES = 2
SIGNS = (1, -1)
SUM1 = ((2, 2, 2, 2), (1, 2, 2, 2))
GATHER = ((2, 2, 2, 2), (2, 2, 2, 1))
SUM2 = ((2, 2, 2, 2), (1, 2, 2, 2))
DEPTH = 4
LAG = 0


def dot(a, b):
    return jnp.dot(a, b, preferred_element_type=F32)


def dot_t(a, b):
    return lax.dot_general(a, b, (((1,), (1,)), ((), ())), preferred_element_type=F32)


def layer_norm(values, gain):
    mean = jnp.mean(values, axis=-1, keepdims=True)
    centered = values - mean
    variance = jnp.mean(centered * centered, axis=-1, keepdims=True)
    return centered * lax.rsqrt(variance + 1e-06) * gain


def positions(hops):
    left, places = sum(hops), []
    for hop in hops:
        places.append(left)
        left -= hop
    return places


class Reduce:
    def __init__(self, me, ring, sides, own, rounded, relay, got, send_sem, recv_sem):
        self.me, self.ring, self.sides = me, ring, sides
        self.places = [positions(hops) for hops in sides]
        self.own, self.rounded, self.relay = own, rounded, relay
        self.got = got
        self.send_sem, self.recv_sem = send_sem, recv_sem
        self.steps = max(len(hops) for hops in sides)

    def place(self, steps):
        return lax.rem(self.me + (steps + self.ring), self.ring)

    def far(self, d, k):
        source = self.relay.at[d, k] if k else self.rounded.at[self.place(self.places[d][0] * SIGNS[d])]
        return pltpu.make_async_remote_copy(
            src_ref=source, dst_ref=self.got.at[k, d],
            send_sem=self.send_sem, recv_sem=self.recv_sem.at[k],
            device_id={"tensor": self.place(self.sides[d][k] * SIGNS[d])}, device_id_type=MESH)

    def has_near(self, d, k):
        return k < len(self.sides[d]) and self.sides[d][k] == 2

    def near_slot(self, d, k):
        return 2 + sum(self.has_near(other, k) for other in range(d))

    def near(self, d, k):
        return pltpu.make_async_remote_copy(
            src_ref=self.rounded.at[self.place((self.places[d][k] - 1) * SIGNS[d])], dst_ref=self.got.at[k, self.near_slot(d, k)],
            send_sem=self.send_sem, recv_sem=self.recv_sem.at[k],
            device_id={"tensor": self.place(SIGNS[d])}, device_id_type=MESH)

    def first(self):
        for d in (0, 1):
            self.far(d, 0).start()
        for k in (0, 1):
            for d in (0, 1):
                if self.has_near(d, k):
                    self.near(d, k).start()

    def arrived(self, k):
        together = self.got.at[k, pl.ds(0, 2 + sum(self.has_near(d, k) for d in (0, 1)))]
        pltpu.make_async_copy(together, together, self.recv_sem.at[k]).wait()
        totals = []
        for d in (0, 1):
            total = self.got[k, d].astype(F32)
            if self.has_near(d, k):
                total = total + self.got[k, self.near_slot(d, k)].astype(F32)
            totals.append(total)
        return totals

    def step(self, k):
        got = self.arrived(k - 1)
        for d in (0, 1):
            mine = self.own[self.place(self.places[d][k] * SIGNS[d])]
            self.relay[d, k] = (mine + got[d]).astype(BF16)
            self.far(d, k).start()
            if self.has_near(d, k + 1):
                self.near(d, k + 1).start()

    def last(self):
        one, other = self.arrived(self.steps - 1)
        return self.own[self.me] + one + other

    def drain(self):
        every = self.rounded.at[pl.ds(0, self.ring - 1)]
        pltpu.make_async_copy(every, every, self.send_sem).wait()


class Gather:
    def __init__(self, me, ring, sides, chunks, send_sem, recv_sem, near_sem):
        self.me, self.ring, self.sides, self.chunks = me, ring, sides, chunks
        self.send_sem, self.recv_sem, self.near_sem = send_sem, recv_sem, near_sem
        self.steps = max(len(hops) for hops in sides)

    def place(self, steps):
        return lax.rem(self.me + (steps + self.ring), self.ring)

    def copy(self, d, k, hop, distance):
        chunk = self.chunks.at[self.place(-distance * SIGNS[d])]
        return pltpu.make_async_remote_copy(
            src_ref=chunk, dst_ref=chunk, send_sem=self.send_sem,
            recv_sem=self.near_sem if hop < self.sides[d][k] else self.recv_sem.at[k],
            device_id={"tensor": self.place(hop * SIGNS[d])}, device_id_type=MESH)

    def sent(self, d, k, hop):
        return self.copy(d, k, hop, sum(self.sides[d][:k]))

    def landed(self):
        return self.chunks.at[pl.ds(0, 2)]

    def step(self, k):
        if k > 0:
            pltpu.make_async_copy(self.landed(), self.landed(), self.recv_sem.at[k - 1]).wait()
        for d in (0, 1):
            self.sent(d, k, self.sides[d][k]).start()
        for d in (0, 1):
            if self.sides[d][k] == 2:
                self.sent(d, k, 1).start()

    def last(self):
        pltpu.make_async_copy(self.landed(), self.landed(), self.recv_sem.at[self.steps - 1]).wait()
        between = self.chunks.at[pl.ds(0, sum(hops.count(2) for hops in self.sides))]
        pltpu.make_async_copy(between, between, self.near_sem).wait()

    def drain(self):
        every = self.chunks.at[pl.ds(0, self.ring - 1)]
        pltpu.make_async_copy(every, every, self.send_sem).wait()


def kernel(
    live_hbm, owner_hbm, vit_gain_hbm, merge_gain_hbm, patches_hbm, fc1_hbm, fc2_hbm, mid_hbm, proj_hbm,
    out_ref,
    live_ref, owner_ref, vit_gain_ref, merge_gain_ref, patches_ref, fc1_ref, fc2_ref, mid_w, proj_w,
    rows, own1, round1, relay1, got1, chunks, own2, round2, relay2, got2,
    outgoing, incoming,
    load_sem, send1, recv1, send_g, recv_g, near_g, send2, recv2, send_x, recv_x,
):
    ring = lax.axis_size("tensor")
    ndp = lax.axis_size("dp")
    me = lax.axis_index("tensor")
    here = lax.axis_index("dp")
    merged = patches_ref.shape[0] // 4
    count = merged // STAGES
    width = patches_ref.shape[1]
    part = width // HALVES
    emb = own2.shape[4]

    barrier = pltpu.get_barrier_semaphore()
    for hops in (1, 2, ring - 2, ring - 1):
        pl.semaphore_signal(barrier, inc=1, device_id={"tensor": lax.rem(me + hops, ring)}, device_id_type=MESH)
    half = patches_ref.shape[0] // STAGES
    loads = [
        pltpu.make_async_copy(source, target, load_sem.at[i])
        for i, (source, target) in enumerate((
            (patches_hbm.at[pl.ds(0, half)], patches_ref.at[pl.ds(0, half)]), (vit_gain_hbm, vit_gain_ref),
            (fc1_hbm, fc1_ref), (fc2_hbm, fc2_ref),
            (patches_hbm.at[pl.ds(half, half)], patches_ref.at[pl.ds(half, half)]), (merge_gain_hbm, merge_gain_ref),
            (mid_hbm, mid_w), (proj_hbm, proj_w), (owner_hbm, owner_ref), (live_hbm, live_ref)))
    ]
    for load in loads[:4]:
        load.start()

    def other(i):
        return lax.rem(here + 1 + lax.rem(i + ndp * 3 // 8, ndp - 1), ndp)

    def greet(i, carry):
        pl.semaphore_signal(barrier, inc=1, device_id={"dp": other(i)}, device_id_type=MESH)
        return carry

    lax.fori_loop(0, ndp - 1, greet, 0)

    def mlp(s):
        total = 4 * count
        to = lax.broadcasted_iota(jnp.int32, (total, total), 0)
        source = lax.broadcasted_iota(jnp.int32, (total, total), 1)
        order = (source == 4 * (to % count) + to // count).astype(BF16)
        ordered = dot(order, patches_ref[s * total : (s + 1) * total, :])
        rows[s] = ordered.astype(BF16).reshape(rows.shape[1:])
        normed = layer_norm(ordered, vit_gain_ref[...].reshape(1, width)).astype(BF16)
        up = dot_t(normed, fc1_ref[...])
        hidden = (up * jax.nn.sigmoid(1.702 * up)).astype(BF16)
        for h in range(HALVES):
            partial = dot(hidden, fc2_ref[:, h * part : (h + 1) * part]).reshape(own1.shape[2:])
            own1[s, h] = partial
            round1[s, h] = partial.astype(BF16)

    stages, halves = range(STAGES), range(HALVES)

    def turned(sides, chain):
        return sides if chain[1] % 2 == 0 else sides[::-1]

    chains = [(s, h) for s in stages for h in halves]
    sums1 = {
        c: Reduce(me, ring, turned(SUM1, c), own1.at[c], round1.at[c], relay1.at[c], got1.at[c], send1.at[c], recv1.at[c])
        for c in chains
    }
    gathers = {c: Gather(me, ring, turned(GATHER, c), chunks.at[c], send_g.at[c], recv_g.at[c], near_g.at[c]) for c in chains}
    sums2 = {
        c: Reduce(me, ring, turned(SUM2, c), own2.at[c], round2.at[c], relay2.at[c], got2.at[c], send2.at[c], recv2.at[c])
        for c in chains
    }

    for load in loads[:4]:
        load.wait()
    for load in loads[4:]:
        load.start()

    def start_sum1(s):
        if s == 1:
            for load in loads[4:6]:
                load.wait()
        mlp(s)
        if s == 0:
            pl.semaphore_wait(barrier, 4 + ndp - 1)
        for h in halves:
            sums1[s, h].first()

    def start_gather(s):
        summed = jnp.concatenate([sums1[s, h].last() for h in halves], axis=1)
        vit_out = (rows[s, me].astype(F32) + summed).astype(BF16)
        normed = layer_norm(vit_out.astype(F32), merge_gain_ref[...].reshape(1, width)).astype(BF16)
        for h in halves:
            chunks[s, h, me] = normed[:, h * part : (h + 1) * part]
            gathers[s, h].step(0)

    def start_sum2(s):
        if s == 0:
            for load in loads[6:]:
                load.wait()
        quarter = ring // 4
        turned_mid = jnp.zeros((mid_w.shape[0], count), F32)
        for h in halves:
            gathers[s, h].last()
            for j in range(4):
                block = chunks[s, h, quarter * j : quarter * (j + 1)].reshape(count, part)
                first = j * width + h * part
                turned_mid = turned_mid + dot_t(mid_w[:, first : first + part], block)
        middle = turned_mid.T
        middle = (0.5 * middle * (1.0 + lax.erf(middle * 0.7071067811865476))).astype(BF16)
        for t in range(ring):
            term = dot(middle, proj_w[:, t * emb : (t + 1) * emb])
            for h in halves:
                piece = term[h * (count // HALVES) : (h + 1) * (count // HALVES)]
                own2[s, h, t] = piece
                round2[s, h, t] = piece.astype(BF16)
        for h in halves:
            sums2[s, h].first()

    def steps_of(group, s):
        def advance(k):
            for h in halves:
                group[s, h].step(k)

        return [functools.partial(advance, k) for k in range(1, group[s, 0].steps)]

    events = [
        [functools.partial(start_sum1, s)] + steps_of(sums1, s)
        + [functools.partial(start_gather, s)] + steps_of(gathers, s)
        + [functools.partial(start_sum2, s)] + steps_of(sums2, s)
        for s in stages
    ]
    for turn in range(len(events[0]) + LAG * (STAGES - 1)):
        for s in stages:
            if 0 <= turn - LAG * s < len(events[s]):
                events[s][turn - LAG * s]()

    owner = jnp.broadcast_to(owner_ref[...], (merged, merged))
    across = lax.broadcasted_iota(jnp.int32, (merged, merged), 1)
    down = lax.broadcasted_iota(jnp.int32, (merged, merged), 0)
    own_col = owner.astype(F32).T.astype(jnp.int32)
    slot = jnp.sum(jnp.where((owner == own_col) & (down < across), 1.0, 0.0), axis=0, keepdims=True)
    column = lax.broadcasted_iota(jnp.int32, (ndp, merged), 1)
    target = lax.broadcasted_iota(jnp.int32, (ndp, merged), 0)
    kept = (owner[:1] == target) & (column * 4 // (4 * merged // 4) < live_ref[0])
    placing = [jnp.where(kept & (slot == float(k)), 1.0, 0.0).astype(BF16) for k in (0, 1)]

    final = jnp.concatenate([sums2[c].last().astype(BF16) for c in chains], axis=0)
    lanes = outgoing.shape[2]
    for k in (0, 1):
        placed = dot(placing[k], final)
        for h in range(emb // lanes):
            outgoing[:, 2 * k + h, :] = placed[:, h * lanes : (h + 1) * lanes]

    def send(i, carry):
        peer = other(i)
        pltpu.make_async_remote_copy(
            src_ref=outgoing.at[peer], dst_ref=incoming.at[here], send_sem=send_x, recv_sem=recv_x,
            device_id={"dp": peer}, device_id_type=MESH).start()
        return carry

    lax.fori_loop(0, ndp - 1, send, 0)
    incoming[here] = outgoing[here]
    for c in chains:
        sums1[c].drain()
        gathers[c].drain()
        sums2[c].drain()
    others = pl.ds(0, ndp - 1)
    pltpu.make_async_copy(outgoing.at[others], incoming.at[others], send_x).wait()
    pltpu.make_async_copy(outgoing.at[others], incoming.at[others], recv_x).wait()

    row = lax.broadcasted_iota(jnp.int32, (2 * ndp, ndp), 0)
    origin = lax.broadcasted_iota(jnp.int32, (2 * ndp, ndp), 1)
    result = jnp.zeros((2 * ndp, emb), F32)
    for k in (0, 1):
        part = jnp.concatenate([incoming[:, 2 * k + h, :] for h in range(emb // lanes)], axis=1).astype(BF16)
        result = result + dot((row == 2 * origin + k).astype(BF16), part)
    out_ref[...] = result.astype(BF16)


def solution(mesh):
    ring, ndp = mesh.shape["tensor"], mesh.shape["dp"]

    def body(patches, live, owners, vit_gain, fc1, fc2, merge_gain, mid, proj):
        total, width = patches.shape
        chunk = total // STAGES // ring
        count = total // 4 // STAGES
        emb = proj.shape[1] // ring
        part, rows = width // HALVES, count // HALVES
        lead = (STAGES, HALVES)
        return pl.pallas_call(
            kernel,
            out_shape=jax.ShapeDtypeStruct((2 * ndp, emb), BF16),
            in_specs=[pl.BlockSpec(memory_space=pl.ANY)] * 9,
            out_specs=pl.BlockSpec(memory_space=pltpu.VMEM),
            scratch_shapes=[
                pltpu.SMEM((1,), jnp.int32),
                pltpu.VMEM((1, total // 4), jnp.int32),
                pltpu.VMEM((width,), F32),
                pltpu.VMEM((width,), F32),
                pltpu.VMEM(patches.shape, BF16),
                pltpu.VMEM(fc1.shape[::-1], BF16),
                pltpu.VMEM(fc2.shape, BF16),
                pltpu.VMEM(mid.shape[::-1], BF16),
                pltpu.VMEM(proj.shape, BF16),
                pltpu.VMEM((STAGES, ring, chunk, width), BF16),
                pltpu.VMEM(lead + (ring, chunk, part), F32),
                pltpu.VMEM(lead + (ring, chunk, part), BF16),
                pltpu.VMEM(lead + (2, DEPTH, chunk, part), BF16),
                pltpu.VMEM(lead + (DEPTH, 4, chunk, part), BF16),
                pltpu.VMEM(lead + (ring, chunk, part), BF16),
                pltpu.VMEM(lead + (ring, rows, emb), F32),
                pltpu.VMEM(lead + (ring, rows, emb), BF16),
                pltpu.VMEM(lead + (2, DEPTH, rows, emb), BF16),
                pltpu.VMEM(lead + (DEPTH, 4, rows, emb), BF16),
                pltpu.VMEM((ndp, 2 * emb // 128, 128), F32),
                pltpu.VMEM((ndp, 2 * emb // 128, 128), F32),
                pltpu.SemaphoreType.DMA((10,)),
            ]
            + [pltpu.SemaphoreType.DMA(lead), pltpu.SemaphoreType.DMA(lead + (DEPTH,))] * 2
            + [pltpu.SemaphoreType.DMA(lead)] * 2
            + [pltpu.SemaphoreType.DMA(lead + (DEPTH,))]
            + [pltpu.SemaphoreType.DMA, pltpu.SemaphoreType.DMA],
            compiler_params=pltpu.CompilerParams(
                collective_id=0, has_side_effects=True, vmem_limit_bytes=56 * 2**20
            ),
            name="vision_block",
        )(live, owners.reshape(1, total // 4), vit_gain, merge_gain, patches, fc1.T, fc2, mid.T, proj)

    return jax.shard_map(
        body,
        mesh=mesh,
        in_specs=(
            P("dp", None), P("dp"), P("dp", None), P(), P(None, "tensor"), P("tensor", None), P(),
            P(None, "tensor"), P("tensor", None),
        ),
        out_specs=P("dp", "tensor"),
        check_vma=False,
    )
```
